32 devices in a mesh: ctx: 16 (over z, x, core), mp: 2 (over y).
Axes of the slice: x: 2, y: 2, z: 4, core: 2. Of those that a mesh axis runs over, the one named last changes fastest.
Arguments:
- hidden: bfloat16 [32768, 512], P('ctx', 'mp'), may hold values from -6 to 6
- w_x: bfloat16 [512, 1024], P(None, 'mp'), may hold values from -0.25 to 0.25
- w_z: bfloat16 [512, 1024], P(None, 'mp'), may hold values from -0.25 to 0.25
- w_bc: bfloat16 [512, 256], replicated, may hold values from -0.25 to 0.25
- w_dt: bfloat16 [512, 16], P(None, 'mp'), may hold values from -0.25 to 0.25
- conv_x: float32 [4, 1024], P(None, 'mp'), may hold values from -3 to 3
- conv_bc: float32 [4, 256], replicated, may hold values from -3 to 3
- dt_bias: float32 [16], P('mp'), may hold values from -5 to -3
- decay_rate: float32 [16], P('mp'), may hold values from 2e-06 to 2
- skip_gain: float32 [16], P('mp'), may hold values from 0.1 to 1.9
- norm_gain: float32 [1024], P('mp'), may hold values from 0.1 to 1.9
- w_out: bfloat16 [1024, 512], P('mp'), may hold values from -0.1875 to 0.1875
- piece_lengths: int32 [4], replicated, may hold values from 1 to 16384, 32768 in all
Outputs:
- layer_out: bfloat16 [32768, 512], P('ctx', 'mp')
The draws below stay inside these ranges and needn't reach their ends.
Inputs may be any that keep to these rules, and one draw needn't show every extreme that they name: `piece_lengths`: the piece lengths add up to 32768, and the longest is exactly 16384.
All inputs are finite; a program needn't handle non-finite values.
Results may differ from the reference program's by a relative error of at most 0.015.
Values may be sent and summed in bfloat16 or wider, within the bound.
A program may use at most 128 MiB of HBM per device.

```python
import math
import jax
import jax.numpy as jnp
import numpy as np
from jax import lax

D = 512
E = 1024
HEAD_DIM = 64
HEADS = 16
NSTATE = 128
BLOCK = 256
TOK_DEV = 2048
TOKENS = 32768
PIECES = 4
MOST = 16384


def draw_hidden(key, part):
    key = jax.random.fold_in(key, 11)
    key_noise = jax.random.fold_in(key, 1)
    key_offset = jax.random.fold_in(key, 2)
    block_total = TOKENS // TOK_DEV
    offset = 0.4 * jax.random.normal(key_offset, (block_total, 1, D), jnp.float32)
    noise = jax.random.normal(key_noise, (block_total, TOK_DEV, D), jnp.float32)
    values = jnp.clip(noise + offset, -6.0, 6.0)
    return values.reshape(TOKENS, D).astype(jnp.bfloat16)


def block_scale(own_key, extent, pieces, least, high):
    level = 1.0
    for dim, blocks in pieces:
        steps = jax.random.uniform(jax.random.fold_in(jax.random.fold_in(own_key, 6), dim), (blocks,), jnp.float32, least / len(pieces), high / len(pieces))
        level = level * jnp.repeat(jnp.exp(steps), extent[dim] // blocks).reshape((-1,) + (1,) * (len(extent) - 1 - dim))
    return level


def profile(count, total, reach, lean):
    portions = [(1 << 20) // math.isqrt(grade ** lean) + 1 for grade in range(2, count + 1)]
    surplus, counts = total - reach - (count - 1), [1] * (count - 1)
    while surplus > 0:
        movable = [i for i in range(count - 1) if counts[i] < reach]
        mass, remaining = sum([portions[i] for i in movable]), surplus
        for i in movable:
            more = min(reach - counts[i], max(1, remaining * portions[i] // mass), surplus)
            counts[i] = counts[i] + more
            surplus = surplus - more
    return np.array([reach] + counts)


def uneven(own_key, number_of, total, most, lean):
    if number_of == 2:
        one = jax.random.randint(own_key, (), max(1, total - most), min(most, total - 1) + 1)
        return jnp.stack([one, total - one])
    tallies = jnp.asarray(profile(number_of, total, most, lean), jnp.int32)
    pairs = (number_of - 1) // 2
    donor, taker = tallies[1:1 + 2 * pairs:2], tallies[2:2 + 2 * pairs:2]
    room = jnp.minimum(donor - 1, most - taker)
    moved = jax.random.randint(jax.random.fold_in(own_key, 1), (pairs,), 0, 1 << 20) % (room + 1)
    tallies = tallies.at[1:1 + 2 * pairs:2].set(donor - moved).at[2:2 + 2 * pairs:2].set(taker + moved)
    return tallies[jax.random.permutation(jax.random.fold_in(own_key, 2), number_of)]


def gaussian(rng, dims, spread, most, cuts=(), held_as=jnp.bfloat16):
    factor_of = block_scale(rng, dims, cuts, -0.22, 0.18) if cuts else 1.0
    result = jax.random.normal(rng, dims, jnp.float32) * spread * factor_of
    return jnp.minimum(jnp.maximum(result, -most), most).astype(held_as)


def setup_inputs(seed: int = 0) -> dict:
    seeds = jax.random.split(jax.random.key(seed), 14)
    return {
        "hidden": draw_hidden(jax.random.fold_in(seeds[13], 71), 0),
        "w_x": gaussian(seeds[1], (D, E), D ** -0.5, 0.25, ((1, 2),)),
        "w_z": gaussian(seeds[2], (D, E), D ** -0.5, 0.25, ((1, 2),)),
        "w_bc": gaussian(seeds[3], (D, 2 * NSTATE), D ** -0.5, 0.25),
        "w_dt": gaussian(seeds[4], (D, HEADS), D ** -0.5, 0.25, ((1, 2),)),
        "conv_x": gaussian(seeds[5], (4, E), 4 ** -0.5, 3.0, ((1, 2),), jnp.float32),
        "conv_bc": gaussian(seeds[6], (4, 2 * NSTATE), 4 ** -0.5, 3.0, (), jnp.float32),
        "dt_bias": jnp.clip(-5.0 + 2.0 * jax.random.uniform(seeds[7], (HEADS,), jnp.float32) ** block_scale(seeds[7], (HEADS,), ((0, 2),), -0.2, 0.2), -5.0, -3.0),
        "decay_rate": jnp.clip(jnp.exp(math.log(2.0) - 13.815511 * jax.random.uniform(seeds[8], (HEADS,), jnp.float32) ** block_scale(seeds[8], (HEADS,), ((0, 2),), -0.2, 0.2)), 1.9999999949504854e-06, 2.0),
        "skip_gain": jnp.clip(1.0 + 0.18 * jax.random.normal(seeds[9], (HEADS,), jnp.float32), 0.1, 1.9),
        "norm_gain": jnp.clip(1.0 + 0.18 * jax.random.normal(seeds[10], (E,), jnp.float32), 0.1, 1.9),
        "w_out": gaussian(seeds[11], (E, D), E ** -0.5, 0.1875, ((0, 2),)),
        "piece_lengths": uneven(seeds[12], PIECES, TOKENS, MOST, 2).astype(jnp.int32),
    }


HIGHEST_PREC = lax.Precision.HIGHEST
EPSILON = 1e-05

def piece_ids(first_pos, length, piece_lengths):
    boundary = jnp.cumsum(piece_lengths).astype(jnp.int32)
    position = first_pos + jnp.arange(length, dtype=jnp.int32)
    return lax.optimization_barrier(jnp.sum((position[:, None] >= boundary[None, :]).astype(jnp.int32), axis=1)).astype(jnp.int32)

def conv_pieces(conv_in, window_seg, conv_w):
    row_count = conv_in.shape[0] - 3
    summed = jnp.zeros((row_count, conv_in.shape[1]), jnp.float32)
    for tap_index in range(4):
        same_piece = (window_seg[tap_index:tap_index + row_count] == window_seg[3:]).astype(jnp.float32)
        summed = summed + conv_in[tap_index:tap_index + row_count].astype(jnp.float32) * conv_w[tap_index][None, :].astype(jnp.float32) * same_piece[:, None]
    return jax.nn.silu(summed).astype(jnp.bfloat16)

def scan_block(carry_state, inputs_x, b_rows, c_rows, step_dt, decay_rate, block_seg, seg_before):
    width_q = inputs_x.shape[0]
    log_decay = -step_dt * decay_rate[None, :]
    cumulated = jnp.cumsum(log_decay, axis=0)
    position = jnp.arange(width_q)
    causal = (block_seg[:, None] == block_seg[None, :]) & (position[:, None] >= position[None, :])
    scores = jnp.dot(c_rows, b_rows.T, preferred_element_type=jnp.float32)
    by_head = cumulated.T
    log_gap = by_head[:, :, None] - by_head[:, None, :]
    decays = jnp.where(causal[None], jnp.exp(jnp.where(causal[None], log_gap, 0.0)), 0.0)
    block_weights = (decays * scores[None] * step_dt.T[:, None, :]).astype(jnp.bfloat16)
    intra_part = jnp.einsum('hts,shp->thp', block_weights.astype(jnp.float32), inputs_x.astype(jnp.float32), precision=HIGHEST_PREC)
    from_start = jnp.exp(cumulated) * (block_seg == seg_before).astype(jnp.float32)[:, None]
    c_scaled = c_rows.astype(jnp.float32)[:, None, :] * from_start[:, :, None]
    inter_part = jnp.einsum('thn,hpn->thp', c_scaled, carry_state, precision=HIGHEST_PREC)
    to_end = jnp.exp(cumulated[-1][None, :] - cumulated) * (block_seg == block_seg[-1]).astype(jnp.float32)[:, None] * step_dt
    state_weights = (b_rows.astype(jnp.float32)[:, None, :] * to_end[:, :, None]).astype(jnp.bfloat16)
    state_added = jnp.einsum('shn,shp->hpn', state_weights.astype(jnp.float32), inputs_x.astype(jnp.float32), precision=HIGHEST_PREC)
    whole_decay = jnp.exp(cumulated[-1]) * (block_seg[-1] == seg_before).astype(jnp.float32)
    new_state = whole_decay[:, None, None] * carry_state + state_added
    return (new_state, intra_part + inter_part, cumulated)

def run_stream(stream_rows, stream_seg, w_in, conv_w, dt_bias, decay_rate, skip_gain, norm_gain, w_out):
    padded = jnp.concatenate([jnp.zeros((3, D), jnp.bfloat16), stream_rows], axis=0)
    seg_pad = jnp.concatenate([jnp.full((3,), -1, jnp.int32), stream_seg.astype(jnp.int32)], axis=0)
    mixing = E + 2 * NSTATE

    def advance(carry_state, block_index):
        offset = (block_index * BLOCK).astype(jnp.int32)
        window = lax.dynamic_slice_in_dim(padded, offset, BLOCK + 3, 0)
        window_seg = lax.dynamic_slice_in_dim(seg_pad, offset, BLOCK + 3, 0)
        projected = jnp.dot(window, w_in, preferred_element_type=jnp.float32).astype(jnp.bfloat16)
        conv_out = conv_pieces(projected[:, :mixing], window_seg, conv_w)
        gate_in = projected[3:, mixing:mixing + E]
        raw_dt = projected[3:, mixing + E:]
        step_dt = jax.nn.softplus(raw_dt.astype(jnp.float32) + dt_bias[None, :])
        inputs_x = conv_out[:, :E].reshape(BLOCK, HEADS, HEAD_DIM)
        b_rows = conv_out[:, E:E + NSTATE]
        c_rows = conv_out[:, E + NSTATE:]
        new_state, mixed_heads, cumulated = scan_block(carry_state, inputs_x, b_rows, c_rows, step_dt, decay_rate, window_seg[3:], window_seg[2])
        mixed_heads = mixed_heads + skip_gain[None, :, None] * inputs_x.astype(jnp.float32)
        gated = mixed_heads.reshape(BLOCK, E) * jax.nn.silu(gate_in.astype(jnp.float32))
        normed = (gated * lax.rsqrt(lax.optimization_barrier(jnp.mean(gated * gated, axis=1, keepdims=True)) + EPSILON) * norm_gain[None, :]).astype(jnp.bfloat16)
        return (new_state, jnp.dot(normed, w_out, preferred_element_type=jnp.float32))
    start_state = jnp.zeros((HEADS, HEAD_DIM, NSTATE), jnp.float32)
    final_state, outputs = lax.scan(advance, start_state, jnp.arange(TOKENS // BLOCK, dtype=jnp.int32))
    return outputs.reshape(TOKENS, D)

def reference(hidden, w_x, w_z, w_bc, w_dt, conv_x, conv_bc, dt_bias, decay_rate, skip_gain, norm_gain, w_out, piece_lengths):
    w_in = jnp.concatenate([w_x, w_bc, w_z, w_dt], axis=1)
    conv_w = jnp.concatenate([conv_x, conv_bc], axis=1)
    seq_piece = piece_ids(0, TOKENS, piece_lengths)
    forward = run_stream(hidden, seq_piece, w_in, conv_w, dt_bias, decay_rate, skip_gain, norm_gain, w_out)
    backward = run_stream(hidden[::-1, ::-1], seq_piece[::-1], w_in, conv_w, dt_bias, decay_rate, skip_gain, norm_gain, w_out)
    return (forward + backward[::-1, ::-1]).astype(jnp.bfloat16)
```

```python
import functools
import jax
import jax.numpy as jnp
from jax import lax
from jax.experimental import pallas as pl
from jax.experimental.pallas import tpu as pltpu
from jax.sharding import PartitionSpec as P

HEAD_DIM = 64
NSTATE = 128
SUB = 128
CHUNK = 256
EPSILON = 1e-05
LOG2E = 1.4426950408889634
F32 = jnp.float32
BF16 = jnp.bfloat16
BIG = 1 << 30
VMEM_LIMIT = 48 * 1024 * 1024

NT = (((1,), (1,)), ((), ()))
TN = (((0,), (0,)), ((), ()))


def piece_start(sm, pieces, pos):
    out = jnp.zeros_like(pos)
    for k in range(pieces):
        bound = sm[k]
        out = jnp.maximum(out, jnp.where(pos >= bound, bound, 0))
    return out


def piece_end(sm, pieces, pos):
    out = jnp.full_like(pos, BIG)
    for k in range(pieces):
        bound = sm[k]
        out = jnp.minimum(out, jnp.where(pos < bound, bound, BIG))
    return out


def silu(value):
    half = 0.5 * value
    return half * jnp.tanh(half) + half


def expand_rows(weights, expander2):
    high = weights.astype(BF16)
    low = (weights - high.astype(F32)).astype(BF16)
    both = jnp.concatenate([high, low], axis=0)
    return lax.dot_general(both, expander2, TN, preferred_element_type=F32)


def project_kernel(nc, mp, inner, pieces, *refs):
    sm = refs[0]
    hf, hr, halo = refs[1 : 1 + mp], refs[1 + mp : 1 + 2 * mp], refs[1 + 2 * mp : 1 + 3 * mp]
    (wf, wr, wdt, cw, head_par, e1, e2) = refs[1 + 3 * mp : 8 + 3 * mp]
    outs = refs[8 + 3 * mp : 22 + 3 * mp]
    buf_f, buf_r, st_f, st_r, dec_f, dec_r = refs[22 + 3 * mp :]
    step = pl.program_id(0)
    base = sm[pieces]
    mixing = inner + 2 * NSTATE
    width = wf.shape[0] // mp

    def dots(blocks, weight, columns):
        total = None
        for b in range(mp):
            part = jnp.dot(
                blocks[b], weight[b * width : (b + 1) * width, columns], preferred_element_type=F32
            )
            total = part if total is None else total + part
        return total

    @pl.when(step == 0)
    def _():
        low = dots([h[0:16, :] for h in halo], wf, slice(0, mixing))
        high = dots([h[16:32, :] for h in halo], wr, slice(0, mixing))
        buf_f[0:8, :] = low[8:16].astype(BF16).astype(F32)
        buf_r[CHUNK : CHUNK + 8, :] = high[0:8].astype(BF16).astype(F32)
        st_f[...] = jnp.zeros_like(st_f)
        st_r[...] = jnp.zeros_like(st_r)
        dec_f[...] = jnp.ones_like(dec_f)
        dec_r[...] = jnp.ones_like(dec_r)

    @pl.when(step > 0)
    def _():
        buf_f[0:8, :] = buf_f[CHUNK : CHUNK + 8, :]
        buf_r[CHUNK : CHUNK + 8, :] = buf_r[0:8, :]

    rows = lax.broadcasted_iota(jnp.int32, (SUB, SUB), 0)
    lanes = lax.broadcasted_iota(jnp.int32, (SUB, SUB), 1)
    for forward in (True, False):
        blocks = [h[...] for h in (hf if forward else hr)]
        weight = wf if forward else wr
        buf = buf_f if forward else buf_r
        state, decay = (st_f, dec_f) if forward else (st_r, dec_r)
        x_out, bc_out, z_out, aux_out, before_out = outs[:5] if forward else outs[5:10]
        chunk = step if forward else nc - 1 - step
        first = base + chunk * CHUNK
        own = 8 if forward else 0
        buf[own : own + CHUNK, :] = (
            dots(blocks, weight, slice(0, mixing)).astype(BF16).astype(F32)
        )
        z_out[...] = dots(blocks, weight, slice(mixing, mixing + inner)).astype(BF16)

        raw = None
        lo = 0 if forward else 8
        for b in range(mp):
            part = lax.dot_general(
                wdt[lo : lo + 8, b * width : (b + 1) * width],
                blocks[b],
                NT,
                preferred_element_type=F32,
            )
            raw = part if raw is None else raw + part
        raw = raw.astype(BF16).astype(F32)
        raw = jnp.concatenate([raw[:, :SUB], raw[:, SUB:]], axis=0)
        par = head_par[...]
        shifted = raw + par[0:16]
        step_dt = jnp.maximum(shifted, 0.0) + jnp.log1p(jnp.exp(-jnp.abs(shifted)))
        log_decay = step_dt * par[16:32]
        tri = jnp.where(rows <= lanes if forward else rows >= lanes, 1.0, 0.0).astype(F32)
        cum = jnp.dot(
            log_decay, tri, precision=lax.Precision.HIGHEST, preferred_element_type=F32
        )
        total = cum[:, SUB - 1 : SUB] if forward else cum[:, 0:1]
        block_first = first + SUB * (lax.broadcasted_iota(jnp.int32, (16, SUB), 0) // 8)
        position = block_first + lax.broadcasted_iota(jnp.int32, (16, SUB), 1)
        start = piece_start(sm, pieces, position)
        end = piece_end(sm, pieces, position)
        block_last = block_first + SUB - 1
        if forward:
            to_end_ok = end > block_last
            from_start_ok = start < block_first
            whole_ok = piece_start(sm, pieces, block_last) < block_first
        else:
            to_end_ok = start <= block_first
            from_start_ok = end > block_last + 1
            whole_ok = piece_end(sm, pieces, block_first) > block_last + 1
        to_end = jnp.where(to_end_ok, jnp.exp2(total - cum) * step_dt, 0.0)
        from_start = jnp.where(from_start_ok, jnp.exp2(cum), 0.0)
        whole = jnp.where(whole_ok, jnp.exp2(jnp.broadcast_to(total, cum.shape)), 0.0)
        aux_out[0, 0:16, :] = cum
        aux_out[0, 16:32, :] = cum - jnp.log2(step_dt)
        aux_out[0, 32:48, :] = from_start
        aux_out[0, 48:64, :] = whole

        for b in (0, 1) if forward else (1, 0):
            at = first + b * SUB + rows
            if forward:
                room = at - piece_start(sm, pieces, at)
            else:
                room = piece_end(sm, pieces, at) - 1 - at
            same = [None] + [room >= j for j in (1, 2, 3)]
            r0 = own + b * SUB
            out_rows = slice(b * SUB, (b + 1) * SUB)
            for g in range(mixing // 128):
                cols = slice(g * 128, (g + 1) * 128)
                acc = buf[r0 : r0 + SUB, cols] * cw[3:4, cols]
                for j in (1, 2, 3):
                    off = r0 - j if forward else r0 + j
                    tap = buf[off : off + SUB, cols] * cw[3 - j : 4 - j, cols]
                    acc = acc + jnp.where(same[j], tap, 0.0)
                value = silu(acc).astype(BF16)
                if g * 128 < inner:
                    x_out[out_rows, cols] = value
                else:
                    bc_out[out_rows, slice(g * 128 - inner, g * 128 - inner + 128)] = value
            hb = slice(b * 8, b * 8 + 8)
            weights = expand_rows(to_end[hb], e2[...])
            scaled = (x_out[out_rows, :].astype(F32) * weights).astype(BF16)
            added = lax.dot_general(
                bc_out[out_rows, 0:NSTATE], scaled, TN, preferred_element_type=F32
            )
            grow = jnp.sum(whole[hb, 0:1] * e1[...], axis=0, keepdims=True)
            held = state[...]
            before_out[b] = held.astype(BF16)
            state[...] = held * grow + added
            decay[...] = decay[...] * grow

    outs[10][...] = st_f[...]
    outs[11][...] = st_r[...]
    outs[12][...] = dec_f[...]
    outs[13][...] = dec_r[...]


def intra_kernel(forward, heads, inner, pieces, sm, x_ref, bc_ref, aux_ref, skip_ref, y_ref):
    first = sm[pieces] + pl.program_id(0) * CHUNK
    rows = lax.broadcasted_iota(jnp.int32, (SUB, SUB), 0)
    lanes = lax.broadcasted_iota(jnp.int32, (SUB, SUB), 1)
    left = lanes < HEAD_DIM
    for b in (0, 1):
        at = slice(b * SUB, (b + 1) * SUB)
        begin = first + b * SUB
        if forward:
            mask = (lanes <= rows) & (begin + lanes >= piece_start(sm, pieces, begin + rows))
        else:
            mask = (lanes >= rows) & (begin + lanes < piece_end(sm, pieces, begin + rows))
        scores = lax.dot_general(
            bc_ref[at, NSTATE:], bc_ref[at, 0:NSTATE], NT, preferred_element_type=F32
        )
        cum_t = aux_ref[0, b * 8 : b * 8 + 8, :].T
        cum_s = aux_ref[0, 16 + b * 8 : 16 + b * 8 + 8, :]
        for pair in range(heads // 2):
            cols = slice(pair * 128, (pair + 1) * 128)
            xp = x_ref[at, cols]
            parts = []
            for h in (2 * pair, 2 * pair + 1):
                gap = jnp.where(mask, cum_t[:, h : h + 1] - cum_s[h : h + 1, :], -1e30)
                parts.append((jnp.exp2(gap) * scores).astype(BF16))
            xf = xp.astype(F32)
            stacked = jnp.concatenate(
                [
                    jnp.where(left, xf, 0.0).astype(BF16),
                    jnp.where(left, 0.0, xf).astype(BF16),
                ],
                axis=0,
            )
            mixed = jnp.dot(
                jnp.concatenate(parts, axis=1), stacked, preferred_element_type=F32
            )
            y_ref[at, cols] = mixed + skip_ref[0:1, cols] * xf


def finish_kernel(nc, inner, *refs):
    ins, par = refs[0:12], refs[12:15]
    outs = refs[15:19]
    grown = refs[19:21]
    gain_ref, e1, e2 = par
    step = pl.program_id(0)

    @pl.when(step == 0)
    def _():
        grown[0][...] = jnp.ones_like(grown[0])
        grown[1][...] = jnp.ones_like(grown[1])

    ones = jnp.ones((8, inner), BF16)
    for stream in (0, 1):
        y_ref, z_ref, bc_ref, aux_ref, before_ref, into_ref = ins[stream * 6 : stream * 6 + 6]
        g_out, ss_out = outs[stream * 2 : stream * 2 + 2]
        into = into_ref[...]
        for b in (0, 1) if stream == 0 else (1, 0):
            at = slice(b * SUB, (b + 1) * SUB)
            grow = grown[stream][...]
            state = (before_ref[b].astype(F32) + grow * into).astype(BF16)
            factor = expand_rows(aux_ref[0, 32 + b * 8 : 40 + b * 8, :], e2[...])
            inter = jnp.dot(bc_ref[at, NSTATE:], state, preferred_element_type=F32)
            mixed = y_ref[at, :] + inter * factor
            gated = mixed * silu(z_ref[at, :].astype(F32))
            ss_out[:, at] = lax.dot_general(
                ones, (gated * gated).astype(BF16), NT, preferred_element_type=F32
            )
            g_out[at, :] = (gated * gain_ref[0:1, :]).astype(BF16)
            whole = aux_ref[0, 48 + b * 8 : 56 + b * 8, 0:1]
            grown[stream][...] = grow * jnp.sum(whole * e1[...], axis=0, keepdims=True)


def output_kernel(mp, total_width, ss_ref, gf_ref, gr_ref, wf_ref, wr_ref, *outs):
    factor = lax.rsqrt(ss_ref[...] * (1.0 / total_width) + EPSILON).T
    width = wf_ref.shape[1] // mp
    for k in range(mp):
        cols = slice(k * width, (k + 1) * width)
        part = factor[:, 0:1] * jnp.dot(gf_ref[...], wf_ref[:, cols], preferred_element_type=F32)
        part = part + factor[:, 4:5] * jnp.dot(
            gr_ref[...], wr_ref[:, cols], preferred_element_type=F32
        )
        outs[k][...] = part.astype(outs[k].dtype)


def shift(value, axis, by, wrap):
    count = lax.axis_size(axis)
    if wrap:
        pairs = [(i, (i + by) % count) for i in range(count)]
    else:
        pairs = [(i, i + by) for i in range(count) if 0 <= i + by < count]
    return lax.ppermute(value, axis, pairs)


def pack_state(state, decay):
    high = decay[0:1].astype(BF16)
    low = (decay[0:1] - high.astype(F32)).astype(BF16)
    tail = jnp.concatenate([high, low, jnp.zeros((14, decay.shape[1]), BF16)], axis=0)
    return jnp.concatenate([state.astype(BF16), tail], axis=0)


def unpack_state(packed):
    decay = packed[NSTATE : NSTATE + 1].astype(F32) + packed[NSTATE + 1 : NSTATE + 2].astype(F32)
    return packed[:NSTATE].astype(F32), decay


def prefix_states(states, decays, axis):
    count = lax.axis_size(axis)
    signs = (1, -1)
    cur = [(s, d[0:1]) for s, d in zip(states, decays)]
    window = 1
    while 4 * window < count - 1:
        packed = [pack_state(*c) for c in cur]
        got = [
            [shift(p, axis, sign * window * k, False) for k in (1, 2, 3)]
            for p, sign in zip(packed, signs)
        ]
        new = []
        for (s, d), parts in zip(cur, got):
            for part in parts:
                more, fade = unpack_state(part)
                s, d = s + d * more, d * fade
            new.append((s, d))
        cur = new
        window *= 4
    reach = -(-(count - 1) // window)
    packed = [pack_state(*c) for c in cur]
    got = [
        [shift(p, axis, sign * (1 + window * k), False) for k in range(reach)]
        for p, sign in zip(packed, signs)
    ]
    result = []
    for parts in got:
        s, d = unpack_state(parts[0])
        for part in parts[1:]:
            more, fade = unpack_state(part)
            s, d = s + d * more, d * fade
        result.append(s)
    return result


def cost(flops, size, trans=0):
    return pl.CostEstimate(flops=flops, bytes_accessed=size, transcendentals=trans)


def shards(
    hidden, w_x, w_z, w_bc, w_dt, conv_x, conv_bc, dt_bias, decay_rate, skip_gain, norm_gain,
    w_out, piece_lengths,
):
    mp = lax.axis_size("mp")
    me = lax.axis_index("mp")
    rows, width = hidden.shape
    model = width * mp
    heads = dt_bias.shape[0]
    inner = heads * HEAD_DIM
    mixing = inner + 2 * NSTATE
    pieces = piece_lengths.shape[0]
    nc = rows // CHUNK
    params = pltpu.CompilerParams(vmem_limit_bytes=VMEM_LIMIT)

    blocks = [hidden] + [shift(hidden, "mp", k, True) for k in range(1, mp)]
    halo_own = jnp.concatenate(
        [shift(hidden[rows - 16 :], "ctx", 1, False), shift(hidden[:16], "ctx", -1, False)], axis=0
    )
    halos = [halo_own] + [shift(halo_own, "mp", k, True) for k in range(1, mp)]

    place = jnp.arange(model, dtype=jnp.int32)
    came = lax.rem(me - place // width + mp, mp) * width + lax.rem(place, width)
    columns = jnp.arange(model, dtype=jnp.int32)[None, :]
    pick_f = (came[:, None] == columns).astype(BF16)
    pick_r = (model - 1 - came[:, None] == columns).astype(BF16)
    w_in = jnp.concatenate([w_x, w_bc, w_z], axis=1)
    w_f = jnp.dot(pick_f, w_in, preferred_element_type=F32).astype(BF16)
    w_r = jnp.dot(pick_r, w_in, preferred_element_type=F32).astype(BF16)
    pad = 8 - heads
    dt_pad = jnp.pad(w_dt, ((0, 0), (0, pad)))
    dt_t = lax.dot_general(
        dt_pad,
        jnp.concatenate([pick_f, pick_r], axis=0),
        (((0,), (1,)), ((), ())),
        preferred_element_type=F32,
    ).astype(BF16)
    w_dt2 = jnp.concatenate([dt_t[:, :model], dt_t[:, model:]], axis=0)
    goes = lax.rem(me + place // width, mp) * width + lax.rem(place, width)
    out_f = jnp.dot(
        w_out, (columns.T == goes[None, :]).astype(BF16), preferred_element_type=F32
    ).astype(BF16)
    out_r = jnp.dot(
        w_out, (columns.T == model - 1 - goes[None, :]).astype(BF16), preferred_element_type=F32
    ).astype(BF16)

    bounds = jnp.cumsum(piece_lengths).astype(jnp.int32)
    sm = jnp.concatenate([bounds, (lax.axis_index("ctx") * rows).astype(jnp.int32)[None]])
    conv_w = jnp.pad(jnp.concatenate([conv_x, conv_bc], axis=1), ((0, 4), (0, 0)))
    bias = jnp.pad(dt_bias, (0, pad))
    rate = jnp.pad(-LOG2E * decay_rate, (0, pad))
    head_par = jnp.broadcast_to(
        jnp.concatenate([bias, bias, rate, rate])[:, None], (32, SUB)
    ).astype(F32)
    owner = jnp.arange(inner, dtype=jnp.int32)[None, :] // HEAD_DIM
    e1 = (jnp.arange(8, dtype=jnp.int32)[:, None] == owner).astype(F32)
    e2 = jnp.concatenate([e1, e1], axis=0).astype(BF16)
    skip8 = jnp.broadcast_to(jnp.repeat(skip_gain, HEAD_DIM)[None, :], (8, inner))
    gain8 = jnp.broadcast_to(norm_gain[None, :], (8, inner))

    smem = pl.BlockSpec(memory_space=pltpu.SMEM)

    def whole(shape):
        return pl.BlockSpec(shape, lambda i: (0,) * len(shape))

    def up(cols):
        return pl.BlockSpec((CHUNK, cols), lambda i: (i, 0))

    def down(cols):
        return pl.BlockSpec((CHUNK, cols), lambda i: (nc - 1 - i, 0))

    aux_up = pl.BlockSpec((1, 64, SUB), lambda i: (i, 0, 0))
    aux_down = pl.BlockSpec((1, 64, SUB), lambda i: (nc - 1 - i, 0, 0))
    st_up = pl.BlockSpec((2, NSTATE, inner), lambda i: (i, 0, 0))
    st_down = pl.BlockSpec((2, NSTATE, inner), lambda i: (nc - 1 - i, 0, 0))

    def sds(shape, dtype):
        return jax.ShapeDtypeStruct(shape, dtype)

    stream_shapes = [
        sds((rows, inner), BF16),
        sds((rows, 2 * NSTATE), BF16),
        sds((rows, inner), BF16),
        sds((nc, 64, SUB), F32),
        sds((2 * nc, NSTATE, inner), BF16),
    ]
    made = pl.pallas_call(
        functools.partial(project_kernel, nc, mp, inner, pieces),
        grid=(nc,),
        in_specs=[smem]
        + [up(width)] * mp
        + [down(width)] * mp
        + [whole((32, width))] * mp
        + [
            whole((model, mixing + inner)),
            whole((model, mixing + inner)),
            whole((16, model)),
            whole((8, mixing)),
            whole((32, SUB)),
            whole((8, inner)),
            whole((16, inner)),
        ],
        out_specs=[up(inner), up(2 * NSTATE), up(inner), aux_up, st_up]
        + [down(inner), down(2 * NSTATE), down(inner), aux_down, st_down]
        + [whole((NSTATE, inner))] * 2
        + [whole((8, inner))] * 2,
        out_shape=stream_shapes
        + stream_shapes
        + [sds((NSTATE, inner), F32)] * 2
        + [sds((8, inner), F32)] * 2,
        scratch_shapes=[
            pltpu.VMEM((CHUNK + 8, mixing), F32),
            pltpu.VMEM((CHUNK + 8, mixing), F32),
            pltpu.VMEM((NSTATE, inner), F32),
            pltpu.VMEM((NSTATE, inner), F32),
            pltpu.VMEM((8, inner), F32),
            pltpu.VMEM((8, inner), F32),
        ],
        compiler_params=params,
        cost_estimate=cost(4 * rows * model * (mixing + inner), 20 << 20),
        name="project",
    )(sm, *blocks, *blocks, *halos, w_f, w_r, w_dt2, conv_w, head_par, e1, e2)
    fwd, rev = made[0:5], made[5:10]

    into = prefix_states(made[10:12], made[12:14], "ctx")

    mixed = []
    for forward, parts in ((True, fwd), (False, rev)):
        mixed.append(
            pl.pallas_call(
                functools.partial(intra_kernel, forward, heads, inner, pieces),
                grid=(nc,),
                in_specs=[smem, up(inner), up(2 * NSTATE), aux_up, whole((8, inner))],
                out_specs=up(inner),
                out_shape=sds((rows, inner), F32),
                compiler_params=params,
                cost_estimate=cost(20 * rows * SUB * inner, 8 << 20, rows * SUB * heads),
                name="intra",
            )(sm, parts[0], parts[1], parts[3], skip8)
        )

    finished = pl.pallas_call(
        functools.partial(finish_kernel, nc, inner),
        grid=(nc,),
        in_specs=[up(inner), up(inner), up(2 * NSTATE), aux_up, st_up, whole((NSTATE, inner))]
        + [down(inner), down(inner), down(2 * NSTATE), aux_down, st_down, whole((NSTATE, inner))]
        + [whole((8, inner)), whole((8, inner)), whole((16, inner))],
        out_specs=[
            up(inner),
            pl.BlockSpec((8, CHUNK), lambda i: (0, i)),
            down(inner),
            pl.BlockSpec((8, CHUNK), lambda i: (0, nc - 1 - i)),
        ],
        out_shape=[sds((rows, inner), BF16), sds((8, rows), F32)] * 2,
        scratch_shapes=[pltpu.VMEM((1, inner), F32)] * 2,
        compiler_params=params,
        cost_estimate=cost(4 * rows * NSTATE * inner, 24 << 20),
        name="finish",
    )(
        mixed[0], fwd[2], fwd[1], fwd[3], fwd[4], into[0],
        mixed[1], rev[2], rev[1], rev[3], rev[4], into[1],
        gain8, e1, e2,
    )
    upper = jnp.arange(8, dtype=jnp.int32)[:, None] < 4
    squares = jnp.where(upper, finished[1], finished[3])
    total = squares
    for k in range(1, mp):
        total = total + shift(squares, "mp", k, True)

    parts = pl.pallas_call(
        functools.partial(output_kernel, mp, inner * mp),
        grid=(nc,),
        in_specs=[
            pl.BlockSpec((8, CHUNK), lambda i: (0, i)),
            up(inner),
            up(inner),
            whole((inner, model)),
            whole((inner, model)),
        ],
        out_specs=[up(width)] * mp,
        out_shape=[sds((rows, width), F32)] + [sds((rows, width), BF16)] * (mp - 1),
        compiler_params=params,
        cost_estimate=cost(4 * rows * inner * model, 8 << 20),
        name="output",
    )(total, finished[0], finished[2], out_f, out_r)
    result = parts[0]
    for k in range(1, mp):
        result = result + shift(parts[k], "mp", k, True).astype(F32)
    return result.astype(BF16)


def solution(mesh):
    return jax.shard_map(
        shards,
        mesh=mesh,
        in_specs=(
            P("ctx", "mp"), P(None, "mp"), P(None, "mp"), P(), P(None, "mp"), P(None, "mp"), P(),
            P("mp"), P("mp"), P("mp"), P("mp"), P("mp", None), P(),
        ),
        out_specs=P("ctx", "mp"),
        check_vma=False,
    )
```

```python
import functools
import jax
import jax.numpy as jnp
from jax import lax
from jax.experimental import pallas as pl
from jax.experimental.pallas import tpu as pltpu
from jax.sharding import PartitionSpec as P

HEAD_DIM = 64
NSTATE = 128
SUB = 128
CHUNK = 256
EPSILON = 1e-05
LOG2E = 1.4426950408889634
F32 = jnp.float32
BF16 = jnp.bfloat16
BIG = 1 << 30
VMEM_LIMIT = 48 * 1024 * 1024

NT = (((1,), (1,)), ((), ()))
TN = (((0,), (0,)), ((), ()))


def piece_start(sm, pieces, pos):
    out = jnp.zeros_like(pos)
    for k in range(pieces):
        bound = sm[k]
        out = jnp.maximum(out, jnp.where(pos >= bound, bound, 0))
    return out


def piece_end(sm, pieces, pos):
    out = jnp.full_like(pos, BIG)
    for k in range(pieces):
        bound = sm[k]
        out = jnp.minimum(out, jnp.where(pos < bound, bound, BIG))
    return out


def silu(value):
    half = 0.5 * value
    return half * jnp.tanh(half) + half


def expand_rows(weights, expander2):
    high = weights.astype(BF16)
    low = (weights - high.astype(F32)).astype(BF16)
    both = jnp.concatenate([high, low], axis=0)
    return lax.dot_general(both, expander2, TN, preferred_element_type=F32)


def project_kernel(nc, mp, inner, pieces, *refs):
    sm = refs[0]
    hf, hr, halo = refs[1 : 1 + mp], refs[1 + mp : 1 + 2 * mp], refs[1 + 2 * mp : 1 + 3 * mp]
    (wf, wr, wdt, cw, head_par, e1, e2) = refs[1 + 3 * mp : 8 + 3 * mp]
    outs = refs[8 + 3 * mp : 22 + 3 * mp]
    buf_f, buf_r, st_f, st_r, dec_f, dec_r = refs[22 + 3 * mp :]
    step = pl.program_id(0)
    base = sm[pieces]
    mixing = inner + 2 * NSTATE
    width = wf.shape[0] // mp

    def dots(blocks, weight, columns):
        total = None
        for b in range(mp):
            part = jnp.dot(
                blocks[b], weight[b * width : (b + 1) * width, columns], preferred_element_type=F32
            )
            total = part if total is None else total + part
        return total

    @pl.when(step == 0)
    def _():
        low = dots([h[0:16, :] for h in halo], wf, slice(0, mixing))
        high = dots([h[16:32, :] for h in halo], wr, slice(0, mixing))
        buf_f[0:8, :] = low[8:16].astype(BF16).astype(F32)
        buf_r[CHUNK : CHUNK + 8, :] = high[0:8].astype(BF16).astype(F32)
        st_f[...] = jnp.zeros_like(st_f)
        st_r[...] = jnp.zeros_like(st_r)
        dec_f[...] = jnp.ones_like(dec_f)
        dec_r[...] = jnp.ones_like(dec_r)

    @pl.when(step > 0)
    def _():
        buf_f[0:8, :] = buf_f[CHUNK : CHUNK + 8, :]
        buf_r[CHUNK : CHUNK + 8, :] = buf_r[0:8, :]

    rows = lax.broadcasted_iota(jnp.int32, (SUB, SUB), 0)
    lanes = lax.broadcasted_iota(jnp.int32, (SUB, SUB), 1)
    for forward in (True, False):
        blocks = [h[...] for h in (hf if forward else hr)]
        weight = wf if forward else wr
        buf = buf_f if forward else buf_r
        state, decay = (st_f, dec_f) if forward else (st_r, dec_r)
        x_out, bc_out, z_out, aux_out, before_out = outs[:5] if forward else outs[5:10]
        chunk = step if forward else nc - 1 - step
        first = base + chunk * CHUNK
        own = 8 if forward else 0
        buf[own : own + CHUNK, :] = (
            dots(blocks, weight, slice(0, mixing)).astype(BF16).astype(F32)
        )
        z_out[...] = dots(blocks, weight, slice(mixing, mixing + inner)).astype(BF16)

        raw = None
        lo = 0 if forward else 8
        for b in range(mp):
            part = lax.dot_general(
                wdt[lo : lo + 8, b * width : (b + 1) * width],
                blocks[b],
                NT,
                preferred_element_type=F32,
            )
            raw = part if raw is None else raw + part
        raw = raw.astype(BF16).astype(F32)
        raw = jnp.concatenate([raw[:, :SUB], raw[:, SUB:]], axis=0)
        par = head_par[...]
        shifted = raw + par[0:16]
        step_dt = jnp.maximum(shifted, 0.0) + jnp.log1p(jnp.exp(-jnp.abs(shifted)))
        log_decay = step_dt * par[16:32]
        tri = jnp.where(rows <= lanes if forward else rows >= lanes, 1.0, 0.0).astype(F32)
        cum = jnp.dot(
            log_decay, tri, precision=lax.Precision.HIGHEST, preferred_element_type=F32
        )
        total = cum[:, SUB - 1 : SUB] if forward else cum[:, 0:1]
        block_first = first + SUB * (lax.broadcasted_iota(jnp.int32, (16, SUB), 0) // 8)
        position = block_first + lax.broadcasted_iota(jnp.int32, (16, SUB), 1)
        start = piece_start(sm, pieces, position)
        end = piece_end(sm, pieces, position)
        block_last = block_first + SUB - 1
        if forward:
            to_end_ok = end > block_last
            from_start_ok = start < block_first
            whole_ok = piece_start(sm, pieces, block_last) < block_first
        else:
            to_end_ok = start <= block_first
            from_start_ok = end > block_last + 1
            whole_ok = piece_end(sm, pieces, block_first) > block_last + 1
        to_end = jnp.where(to_end_ok, jnp.exp2(total - cum) * step_dt, 0.0)
        from_start = jnp.where(from_start_ok, jnp.exp2(cum), 0.0)
        whole = jnp.where(whole_ok, jnp.exp2(jnp.broadcast_to(total, cum.shape)), 0.0)
        aux_out[0, 0:16, :] = cum
        aux_out[0, 16:32, :] = cum - jnp.log2(step_dt)
        aux_out[0, 32:48, :] = from_start
        aux_out[0, 48:64, :] = whole

        for b in (0, 1) if forward else (1, 0):
            at = first + b * SUB + rows
            if forward:
                room = at - piece_start(sm, pieces, at)
            else:
                room = piece_end(sm, pieces, at) - 1 - at
            same = [None] + [room >= j for j in (1, 2, 3)]
            r0 = own + b * SUB
            out_rows = slice(b * SUB, (b + 1) * SUB)
            for g in range(mixing // 128):
                cols = slice(g * 128, (g + 1) * 128)
                acc = buf[r0 : r0 + SUB, cols] * cw[3:4, cols]
                for j in (1, 2, 3):
                    off = r0 - j if forward else r0 + j
                    tap = buf[off : off + SUB, cols] * cw[3 - j : 4 - j, cols]
                    acc = acc + jnp.where(same[j], tap, 0.0)
                value = silu(acc).astype(BF16)
                if g * 128 < inner:
                    x_out[out_rows, cols] = value
                else:
                    bc_out[out_rows, slice(g * 128 - inner, g * 128 - inner + 128)] = value
            hb = slice(b * 8, b * 8 + 8)
            weights = expand_rows(to_end[hb], e2[...])
            scaled = (x_out[out_rows, :].astype(F32) * weights).astype(BF16)
            added = lax.dot_general(
                bc_out[out_rows, 0:NSTATE], scaled, TN, preferred_element_type=F32
            )
            grow = jnp.sum(whole[hb, 0:1] * e1[...], axis=0, keepdims=True)
            held = state[...]
            before_out[b] = held.astype(BF16)
            state[...] = held * grow + added
            decay[...] = decay[...] * grow

    outs[10][...] = st_f[...]
    outs[11][...] = st_r[...]
    outs[12][...] = dec_f[...]
    outs[13][...] = dec_r[...]


def intra_rows(forward, heads, pieces, sm, x_ref, bc_ref, aux_ref, skip_ref, y_ref, chunk):
    base = sm[pieces]
    rows = lax.broadcasted_iota(jnp.int32, (SUB, SUB), 0)
    lanes = lax.broadcasted_iota(jnp.int32, (SUB, SUB), 1)
    left = lanes < HEAD_DIM
    aux = aux_ref[chunk]
    for b in (0, 1):
        at = pl.ds(pl.multiple_of(chunk * CHUNK + b * SUB, SUB), SUB)
        begin = base + chunk * CHUNK + b * SUB
        if forward:
            mask = (lanes <= rows) & (begin + lanes >= piece_start(sm, pieces, begin + rows))
        else:
            mask = (lanes >= rows) & (begin + lanes < piece_end(sm, pieces, begin + rows))
        scores = lax.dot_general(
            bc_ref[at, NSTATE:], bc_ref[at, 0:NSTATE], NT, preferred_element_type=F32
        )
        cum_t = aux[b * 8 : b * 8 + 8, :].T
        cum_s = aux[16 + b * 8 : 16 + b * 8 + 8, :]
        for pair in range(heads // 2):
            cols = slice(pair * 128, (pair + 1) * 128)
            xf = x_ref[at, cols].astype(F32)
            parts = []
            for h in (2 * pair, 2 * pair + 1):
                gap = jnp.where(mask, cum_t[:, h : h + 1] - cum_s[h : h + 1, :], -1e30)
                parts.append((jnp.exp2(gap) * scores).astype(BF16))
            stacked = jnp.concatenate(
                [
                    jnp.where(left, xf, 0.0).astype(BF16),
                    jnp.where(left, 0.0, xf).astype(BF16),
                ],
                axis=0,
            )
            mixed = jnp.dot(
                jnp.concatenate(parts, axis=1), stacked, preferred_element_type=F32
            )
            y_ref[at, cols] = (mixed + skip_ref[0:1, cols] * xf).astype(BF16)


def rounds_of(count):
    rounds, window = [], 1
    while 4 * window < count - 1:
        rounds.append([window * k for k in (1, 2, 3)])
        window *= 4
    rounds.append([1 + window * k for k in range(-(-(count - 1) // window))])
    return rounds


def exchange_kernel(count, nc, heads, pieces, *refs):
    sm, st_f, st_r, dec_f, dec_r, x_f, bc_f, aux_f, x_r, bc_r, aux_r, skip = refs[:12]
    y_f, y_r, into_f, into_r = refs[12:16]
    sent, landed, held, fade, send_sem, recv_sem = refs[16:]
    index = lax.axis_index("ctx")
    rounds = rounds_of(count)
    signs = (1, -1)

    def reaches(step):
        return index + step < count if step > 0 else index + step >= 0

    def peer(step):
        return {"ctx": index + step}

    barrier = pltpu.get_barrier_semaphore()
    steps = sorted({sign * s for r in rounds for s in r for sign in signs})
    for step in steps:

        @pl.when(reaches(step))
        def _(step=step):
            pl.semaphore_signal(
                barrier, inc=1, device_id=peer(step), device_id_type=pl.DeviceIdType.MESH
            )

    peers = sum(
        1 - lax.div(index + step, count) if step > 0 else lax.div(index + step + count, count)
        for step in steps
    )
    pl.semaphore_wait(barrier, peers)

    held[0], held[1] = st_f[...], st_r[...]
    fade[0], fade[1] = dec_f[...], dec_r[...]
    jobs = (
        (True, x_f, bc_f, aux_f, y_f),
        (False, x_r, bc_r, aux_r, y_r),
    )
    slot = 0
    for number, shifts in enumerate(rounds):
        last = number == len(rounds) - 1
        copies = []
        for stream, sign in enumerate(signs):
            at = number * 2 + stream
            decay = fade[stream]
            high = decay.astype(BF16)
            low = (decay - high.astype(F32)).astype(BF16)
            sent[at, 0:NSTATE, :] = held[stream].astype(BF16)
            sent[at, NSTATE : NSTATE + 16, :] = jnp.concatenate([high, low], axis=0)
            for s in shifts:
                copy = pltpu.make_async_remote_copy(
                    src_ref=sent.at[at],
                    dst_ref=landed.at[slot],
                    send_sem=send_sem.at[slot],
                    recv_sem=recv_sem.at[slot],
                    device_id=peer(sign * s),
                    device_id_type=pl.DeviceIdType.MESH,
                )
                copies.append((stream, sign * s, slot, copy))
                slot += 1

                @pl.when(reaches(sign * s))
                def _(copy=copy):
                    copy.start()

        if number < len(jobs):
            forward, x_ref, bc_ref, aux_ref, y_ref = jobs[number]

            def body(chunk, carry):
                intra_rows(
                    forward, heads, pieces, sm, x_ref, bc_ref, aux_ref, skip, y_ref, chunk
                )
                return carry

            lax.fori_loop(0, nc, body, 0)

        if last:
            held[...] = jnp.zeros_like(held)
            fade[...] = jnp.ones_like(fade)
        for stream, step, at, copy in copies:

            @pl.when(reaches(-step))
            def _(stream=stream, at=at, copy=copy):
                copy.wait_recv()
                more = landed[at, 0:NSTATE, :].astype(F32)
                tail = landed[at, NSTATE : NSTATE + 16, :].astype(F32)
                held[stream] = held[stream] + fade[stream, 0:1, :] * more
                fade[stream] = fade[stream] * (tail[0:8] + tail[8:16])

        for stream, step, at, copy in copies:

            @pl.when(reaches(step))
            def _(copy=copy):
                copy.wait_send()

    into_f[...] = held[0]
    into_r[...] = held[1]


def finish_kernel(nc, inner, *refs):
    ins, par = refs[0:12], refs[12:15]
    outs = refs[15:19]
    grown = refs[19:21]
    gain_ref, e1, e2 = par
    step = pl.program_id(0)

    @pl.when(step == 0)
    def _():
        grown[0][...] = jnp.ones_like(grown[0])
        grown[1][...] = jnp.ones_like(grown[1])

    ones = jnp.ones((8, inner), BF16)
    for stream in (0, 1):
        y_ref, z_ref, bc_ref, aux_ref, before_ref, into_ref = ins[stream * 6 : stream * 6 + 6]
        g_out, ss_out = outs[stream * 2 : stream * 2 + 2]
        into = into_ref[...]
        for b in (0, 1) if stream == 0 else (1, 0):
            at = slice(b * SUB, (b + 1) * SUB)
            grow = grown[stream][...]
            state = (before_ref[b].astype(F32) + grow * into).astype(BF16)
            factor = expand_rows(aux_ref[0, 32 + b * 8 : 40 + b * 8, :], e2[...])
            inter = jnp.dot(bc_ref[at, NSTATE:], state, preferred_element_type=F32)
            mixed = y_ref[at, :].astype(F32) + inter * factor
            gated = mixed * silu(z_ref[at, :].astype(F32))
            ss_out[:, at] = lax.dot_general(
                ones, (gated * gated).astype(BF16), NT, preferred_element_type=F32
            )
            g_out[at, :] = (gated * gain_ref[0:1, :]).astype(BF16)
            whole = aux_ref[0, 48 + b * 8 : 56 + b * 8, 0:1]
            grown[stream][...] = grow * jnp.sum(whole * e1[...], axis=0, keepdims=True)


def output_kernel(mp, total_width, ss_ref, gf_ref, gr_ref, wf_ref, wr_ref, *outs):
    factor = lax.rsqrt(ss_ref[...] * (1.0 / total_width) + EPSILON).T
    width = wf_ref.shape[1] // mp
    for k in range(mp):
        cols = slice(k * width, (k + 1) * width)
        part = factor[:, 0:1] * jnp.dot(gf_ref[...], wf_ref[:, cols], preferred_element_type=F32)
        part = part + factor[:, 4:5] * jnp.dot(
            gr_ref[...], wr_ref[:, cols], preferred_element_type=F32
        )
        outs[k][...] = part.astype(outs[k].dtype)


def shift(value, axis, by, wrap):
    count = lax.axis_size(axis)
    if wrap:
        pairs = [(i, (i + by) % count) for i in range(count)]
    else:
        pairs = [(i, i + by) for i in range(count) if 0 <= i + by < count]
    return lax.ppermute(value, axis, pairs)


def cost(flops, size, trans=0):
    return pl.CostEstimate(flops=flops, bytes_accessed=size, transcendentals=trans)


def shards(
    hidden, w_x, w_z, w_bc, w_dt, conv_x, conv_bc, dt_bias, decay_rate, skip_gain, norm_gain,
    w_out, piece_lengths,
):
    mp = lax.axis_size("mp")
    me = lax.axis_index("mp")
    rows, width = hidden.shape
    model = width * mp
    heads = dt_bias.shape[0]
    inner = heads * HEAD_DIM
    mixing = inner + 2 * NSTATE
    pieces = piece_lengths.shape[0]
    nc = rows // CHUNK
    params = pltpu.CompilerParams(vmem_limit_bytes=VMEM_LIMIT)

    blocks = [hidden] + [shift(hidden, "mp", k, True) for k in range(1, mp)]
    halo_own = jnp.concatenate(
        [shift(hidden[rows - 16 :], "ctx", 1, False), shift(hidden[:16], "ctx", -1, False)], axis=0
    )
    halos = [halo_own] + [shift(halo_own, "mp", k, True) for k in range(1, mp)]

    place = jnp.arange(model, dtype=jnp.int32)
    came = lax.rem(me - place // width + mp, mp) * width + lax.rem(place, width)
    columns = jnp.arange(model, dtype=jnp.int32)[None, :]
    pick_f = (came[:, None] == columns).astype(BF16)
    pick_r = (model - 1 - came[:, None] == columns).astype(BF16)
    w_in = jnp.concatenate([w_x, w_bc, w_z], axis=1)
    w_f = jnp.dot(pick_f, w_in, preferred_element_type=F32).astype(BF16)
    w_r = jnp.dot(pick_r, w_in, preferred_element_type=F32).astype(BF16)
    pad = 8 - heads
    dt_pad = jnp.pad(w_dt, ((0, 0), (0, pad)))
    dt_t = lax.dot_general(
        dt_pad,
        jnp.concatenate([pick_f, pick_r], axis=0),
        (((0,), (1,)), ((), ())),
        preferred_element_type=F32,
    ).astype(BF16)
    w_dt2 = jnp.concatenate([dt_t[:, :model], dt_t[:, model:]], axis=0)
    goes = lax.rem(me + place // width, mp) * width + lax.rem(place, width)
    out_f = jnp.dot(
        w_out, (columns.T == goes[None, :]).astype(BF16), preferred_element_type=F32
    ).astype(BF16)
    out_r = jnp.dot(
        w_out, (columns.T == model - 1 - goes[None, :]).astype(BF16), preferred_element_type=F32
    ).astype(BF16)

    bounds = jnp.cumsum(piece_lengths).astype(jnp.int32)
    sm = jnp.concatenate([bounds, (lax.axis_index("ctx") * rows).astype(jnp.int32)[None]])
    conv_w = jnp.pad(jnp.concatenate([conv_x, conv_bc], axis=1), ((0, 4), (0, 0)))
    bias = jnp.pad(dt_bias, (0, pad))
    rate = jnp.pad(-LOG2E * decay_rate, (0, pad))
    head_par = jnp.broadcast_to(
        jnp.concatenate([bias, bias, rate, rate])[:, None], (32, SUB)
    ).astype(F32)
    owner = jnp.arange(inner, dtype=jnp.int32)[None, :] // HEAD_DIM
    e1 = (jnp.arange(8, dtype=jnp.int32)[:, None] == owner).astype(F32)
    e2 = jnp.concatenate([e1, e1], axis=0).astype(BF16)
    skip8 = jnp.broadcast_to(jnp.repeat(skip_gain, HEAD_DIM)[None, :], (8, inner))
    gain8 = jnp.broadcast_to(norm_gain[None, :], (8, inner))

    smem = pl.BlockSpec(memory_space=pltpu.SMEM)

    def whole(shape):
        return pl.BlockSpec(shape, lambda i: (0,) * len(shape))

    def up(cols):
        return pl.BlockSpec((CHUNK, cols), lambda i: (i, 0))

    def down(cols):
        return pl.BlockSpec((CHUNK, cols), lambda i: (nc - 1 - i, 0))

    aux_up = pl.BlockSpec((1, 64, SUB), lambda i: (i, 0, 0))
    aux_down = pl.BlockSpec((1, 64, SUB), lambda i: (nc - 1 - i, 0, 0))
    st_up = pl.BlockSpec((2, NSTATE, inner), lambda i: (i, 0, 0))
    st_down = pl.BlockSpec((2, NSTATE, inner), lambda i: (nc - 1 - i, 0, 0))

    def sds(shape, dtype):
        return jax.ShapeDtypeStruct(shape, dtype)

    stream_shapes = [
        sds((rows, inner), BF16),
        sds((rows, 2 * NSTATE), BF16),
        sds((rows, inner), BF16),
        sds((nc, 64, SUB), F32),
        sds((2 * nc, NSTATE, inner), BF16),
    ]
    made = pl.pallas_call(
        functools.partial(project_kernel, nc, mp, inner, pieces),
        grid=(nc,),
        in_specs=[smem]
        + [up(width)] * mp
        + [down(width)] * mp
        + [whole((32, width))] * mp
        + [
            whole((model, mixing + inner)),
            whole((model, mixing + inner)),
            whole((16, model)),
            whole((8, mixing)),
            whole((32, SUB)),
            whole((8, inner)),
            whole((16, inner)),
        ],
        out_specs=[up(inner), up(2 * NSTATE), up(inner), aux_up, st_up]
        + [down(inner), down(2 * NSTATE), down(inner), aux_down, st_down]
        + [whole((NSTATE, inner))] * 2
        + [whole((8, inner))] * 2,
        out_shape=stream_shapes
        + stream_shapes
        + [sds((NSTATE, inner), F32)] * 2
        + [sds((8, inner), F32)] * 2,
        scratch_shapes=[
            pltpu.VMEM((CHUNK + 8, mixing), F32),
            pltpu.VMEM((CHUNK + 8, mixing), F32),
            pltpu.VMEM((NSTATE, inner), F32),
            pltpu.VMEM((NSTATE, inner), F32),
            pltpu.VMEM((8, inner), F32),
            pltpu.VMEM((8, inner), F32),
        ],
        compiler_params=params,
        cost_estimate=cost(4 * rows * model * (mixing + inner), 20 << 20),
        name="project",
    )(sm, *blocks, *blocks, *halos, w_f, w_r, w_dt2, conv_w, head_par, e1, e2)
    fwd, rev = made[0:5], made[5:10]

    count = lax.axis_size("ctx")
    rounds = rounds_of(count)
    slots = 2 * sum(len(r) for r in rounds)
    packed = NSTATE + 16
    vmem = pl.BlockSpec(memory_space=pltpu.VMEM)
    *mixed, into_f, into_r = pl.pallas_call(
        functools.partial(exchange_kernel, count, nc, heads, pieces),
        in_specs=[smem] + [vmem] * 11,
        out_specs=[vmem] * 4,
        out_shape=[sds((rows, inner), BF16)] * 2 + [sds((NSTATE, inner), F32)] * 2,
        scratch_shapes=[
            pltpu.VMEM((2 * len(rounds), packed, inner), BF16),
            pltpu.VMEM((slots, packed, inner), BF16),
            pltpu.VMEM((2, NSTATE, inner), F32),
            pltpu.VMEM((2, 8, inner), F32),
            pltpu.SemaphoreType.DMA((slots,)),
            pltpu.SemaphoreType.DMA((slots,)),
        ],
        compiler_params=pltpu.CompilerParams(
            vmem_limit_bytes=VMEM_LIMIT, collective_id=0, has_side_effects=True
        ),
        cost_estimate=cost(40 * rows * SUB * inner, 16 << 20, 2 * rows * SUB * heads),
        name="exchange",
    )(
        sm, *made[10:14], fwd[0], fwd[1], fwd[3], rev[0], rev[1], rev[3], skip8,
    )
    into = (into_f, into_r)

    finished = pl.pallas_call(
        functools.partial(finish_kernel, nc, inner),
        grid=(nc,),
        in_specs=[up(inner), up(inner), up(2 * NSTATE), aux_up, st_up, whole((NSTATE, inner))]
        + [down(inner), down(inner), down(2 * NSTATE), aux_down, st_down, whole((NSTATE, inner))]
        + [whole((8, inner)), whole((8, inner)), whole((16, inner))],
        out_specs=[
            up(inner),
            pl.BlockSpec((8, CHUNK), lambda i: (0, i)),
            down(inner),
            pl.BlockSpec((8, CHUNK), lambda i: (0, nc - 1 - i)),
        ],
        out_shape=[sds((rows, inner), BF16), sds((8, rows), F32)] * 2,
        scratch_shapes=[pltpu.VMEM((1, inner), F32)] * 2,
        compiler_params=params,
        cost_estimate=cost(4 * rows * NSTATE * inner, 24 << 20),
        name="finish",
    )(
        mixed[0], fwd[2], fwd[1], fwd[3], fwd[4], into[0],
        mixed[1], rev[2], rev[1], rev[3], rev[4], into[1],
        gain8, e1, e2,
    )
    upper = jnp.arange(8, dtype=jnp.int32)[:, None] < 4
    squares = jnp.where(upper, finished[1], finished[3])
    total = squares
    for k in range(1, mp):
        total = total + shift(squares, "mp", k, True)

    parts = pl.pallas_call(
        functools.partial(output_kernel, mp, inner * mp),
        grid=(nc,),
        in_specs=[
            pl.BlockSpec((8, CHUNK), lambda i: (0, i)),
            up(inner),
            up(inner),
            whole((inner, model)),
            whole((inner, model)),
        ],
        out_specs=[up(width)] * mp,
        out_shape=[sds((rows, width), F32)] + [sds((rows, width), BF16)] * (mp - 1),
        compiler_params=params,
        cost_estimate=cost(4 * rows * inner * model, 8 << 20),
        name="output",
    )(total, finished[0], finished[2], out_f, out_r)
    result = parts[0]
    for k in range(1, mp):
        result = result + shift(parts[k], "mp", k, True).astype(F32)
    return result.astype(BF16)


def solution(mesh):
    return jax.shard_map(
        shards,
        mesh=mesh,
        in_specs=(
            P("ctx", "mp"), P(None, "mp"), P(None, "mp"), P(), P(None, "mp"), P(None, "mp"), P(),
            P("mp"), P("mp"), P("mp"), P("mp"), P("mp", None), P(),
        ),
        out_specs=P("ctx", "mp"),
        check_vma=False,
    )
```

```python
import functools
import jax
import jax.numpy as jnp
from jax import lax
from jax.experimental import pallas as pl
from jax.experimental.pallas import tpu as pltpu
from jax.sharding import PartitionSpec as P

HEAD_DIM = 64
NSTATE = 128
SUB = 128
CHUNK = 256
EPSILON = 1e-05
LOG2E = 1.4426950408889634
F32 = jnp.float32
BF16 = jnp.bfloat16
BIG = 1 << 30
VMEM_LIMIT = 48 * 1024 * 1024

NT = (((1,), (1,)), ((), ()))
TN = (((0,), (0,)), ((), ()))


def piece_start(sm, pieces, pos):
    out = jnp.zeros_like(pos)
    for k in range(pieces):
        bound = sm[k]
        out = jnp.maximum(out, jnp.where(pos >= bound, bound, 0))
    return out


def piece_end(sm, pieces, pos):
    out = jnp.full_like(pos, BIG)
    for k in range(pieces):
        bound = sm[k]
        out = jnp.minimum(out, jnp.where(pos < bound, bound, BIG))
    return out


def silu(value):
    half = 0.5 * value
    return half * jnp.tanh(half) + half


def expand_rows(weights, expander2):
    high = weights.astype(BF16)
    low = (weights - high.astype(F32)).astype(BF16)
    both = jnp.concatenate([high, low], axis=0)
    return lax.dot_general(both, expander2, TN, preferred_element_type=F32)


def project_kernel(nc, mp, inner, pieces, *refs):
    sm = refs[0]
    hf, hr, halo = refs[1 : 1 + mp], refs[1 + mp : 1 + 2 * mp], refs[1 + 2 * mp : 1 + 3 * mp]
    (wf, wr, wdt, cw, head_par, e1, e2) = refs[1 + 3 * mp : 8 + 3 * mp]
    outs = refs[8 + 3 * mp : 22 + 3 * mp]
    buf_f, buf_r, st_f, st_r, dec_f, dec_r = refs[22 + 3 * mp :]
    step = pl.program_id(0)
    base = sm[pieces]
    mixing = inner + 2 * NSTATE
    width = wf.shape[0] // mp

    def dots(blocks, weight, columns):
        total = None
        for b in range(mp):
            part = jnp.dot(
                blocks[b], weight[b * width : (b + 1) * width, columns], preferred_element_type=F32
            )
            total = part if total is None else total + part
        return total

    @pl.when(step == 0)
    def _():
        low = dots([h[0:16, :] for h in halo], wf, slice(0, mixing))
        high = dots([h[16:32, :] for h in halo], wr, slice(0, mixing))
        buf_f[0:8, :] = low[8:16].astype(BF16).astype(F32)
        buf_r[CHUNK : CHUNK + 8, :] = high[0:8].astype(BF16).astype(F32)
        st_f[...] = jnp.zeros_like(st_f)
        st_r[...] = jnp.zeros_like(st_r)
        dec_f[...] = jnp.ones_like(dec_f)
        dec_r[...] = jnp.ones_like(dec_r)

    @pl.when(step > 0)
    def _():
        buf_f[0:8, :] = buf_f[CHUNK : CHUNK + 8, :]
        buf_r[CHUNK : CHUNK + 8, :] = buf_r[0:8, :]

    rows = lax.broadcasted_iota(jnp.int32, (SUB, SUB), 0)
    lanes = lax.broadcasted_iota(jnp.int32, (SUB, SUB), 1)
    for forward in (True, False):
        blocks = [h[...] for h in (hf if forward else hr)]
        weight = wf if forward else wr
        buf = buf_f if forward else buf_r
        state, decay = (st_f, dec_f) if forward else (st_r, dec_r)
        x_out, bc_out, z_out, aux_out, before_out = outs[:5] if forward else outs[5:10]
        chunk = step if forward else nc - 1 - step
        first = base + chunk * CHUNK
        own = 8 if forward else 0
        buf[own : own + CHUNK, :] = (
            dots(blocks, weight, slice(0, mixing)).astype(BF16).astype(F32)
        )
        z_out[...] = dots(blocks, weight, slice(mixing, mixing + inner)).astype(BF16)

        raw = None
        lo = 0 if forward else 8
        for b in range(mp):
            part = lax.dot_general(
                wdt[lo : lo + 8, b * width : (b + 1) * width],
                blocks[b],
                NT,
                preferred_element_type=F32,
            )
            raw = part if raw is None else raw + part
        raw = raw.astype(BF16).astype(F32)
        raw = jnp.concatenate([raw[:, :SUB], raw[:, SUB:]], axis=0)
        par = head_par[...]
        shifted = raw + par[0:16]
        step_dt = jnp.maximum(shifted, 0.0) + jnp.log1p(jnp.exp(-jnp.abs(shifted)))
        log_decay = step_dt * par[16:32]
        tri = jnp.where(rows <= lanes if forward else rows >= lanes, 1.0, 0.0).astype(F32)
        cum = jnp.dot(
            log_decay, tri, precision=lax.Precision.HIGHEST, preferred_element_type=F32
        )
        total = cum[:, SUB - 1 : SUB] if forward else cum[:, 0:1]
        block_first = first + SUB * (lax.broadcasted_iota(jnp.int32, (16, SUB), 0) // 8)
        position = block_first + lax.broadcasted_iota(jnp.int32, (16, SUB), 1)
        start = piece_start(sm, pieces, position)
        end = piece_end(sm, pieces, position)
        block_last = block_first + SUB - 1
        if forward:
            to_end_ok = end > block_last
            from_start_ok = start < block_first
            whole_ok = piece_start(sm, pieces, block_last) < block_first
        else:
            to_end_ok = start <= block_first
            from_start_ok = end > block_last + 1
            whole_ok = piece_end(sm, pieces, block_first) > block_last + 1
        to_end = jnp.where(to_end_ok, jnp.exp2(total - cum) * step_dt, 0.0)
        from_start = jnp.where(from_start_ok, jnp.exp2(cum), 0.0)
        whole = jnp.where(whole_ok, jnp.exp2(jnp.broadcast_to(total, cum.shape)), 0.0)
        aux_out[0, 0:16, :] = cum
        aux_out[0, 16:32, :] = cum - jnp.log2(step_dt)
        aux_out[0, 32:48, :] = from_start
        aux_out[0, 48:64, :] = whole

        for b in (0, 1) if forward else (1, 0):
            at = first + b * SUB + rows
            if forward:
                room = at - piece_start(sm, pieces, at)
            else:
                room = piece_end(sm, pieces, at) - 1 - at
            same = [None] + [room >= j for j in (1, 2, 3)]
            r0 = own + b * SUB
            out_rows = slice(b * SUB, (b + 1) * SUB)
            for g in range(mixing // 128):
                cols = slice(g * 128, (g + 1) * 128)
                acc = buf[r0 : r0 + SUB, cols] * cw[3:4, cols]
                for j in (1, 2, 3):
                    off = r0 - j if forward else r0 + j
                    tap = buf[off : off + SUB, cols] * cw[3 - j : 4 - j, cols]
                    acc = acc + jnp.where(same[j], tap, 0.0)
                value = silu(acc).astype(BF16)
                if g * 128 < inner:
                    x_out[out_rows, cols] = value
                else:
                    bc_out[out_rows, slice(g * 128 - inner, g * 128 - inner + 128)] = value
            hb = slice(b * 8, b * 8 + 8)
            weights = expand_rows(to_end[hb], e2[...])
            scaled = (x_out[out_rows, :].astype(F32) * weights).astype(BF16)
            added = lax.dot_general(
                bc_out[out_rows, 0:NSTATE], scaled, TN, preferred_element_type=F32
            )
            grow = jnp.sum(whole[hb, 0:1] * e1[...], axis=0, keepdims=True)
            held = state[...]
            before_out[b] = held.astype(BF16)
            state[...] = held * grow + added
            decay[...] = decay[...] * grow

    outs[10][...] = st_f[...]
    outs[11][...] = st_r[...]
    outs[12][...] = dec_f[...]
    outs[13][...] = dec_r[...]


def intra_rows(forward, heads, pieces, sm, x_ref, bc_ref, aux_ref, skip_ref, y_ref, offset, chunk):
    base = sm[pieces] + offset
    rows = lax.broadcasted_iota(jnp.int32, (SUB, SUB), 0)
    lanes = lax.broadcasted_iota(jnp.int32, (SUB, SUB), 1)
    left = lanes < HEAD_DIM
    aux = aux_ref[chunk]
    for b in (0, 1):
        at = pl.ds(pl.multiple_of(chunk * CHUNK + b * SUB, SUB), SUB)
        begin = base + chunk * CHUNK + b * SUB
        if forward:
            mask = (lanes <= rows) & (begin + lanes >= piece_start(sm, pieces, begin + rows))
        else:
            mask = (lanes >= rows) & (begin + lanes < piece_end(sm, pieces, begin + rows))
        scores = lax.dot_general(
            bc_ref[at, NSTATE:], bc_ref[at, 0:NSTATE], NT, preferred_element_type=F32
        )
        cum_t = aux[b * 8 : b * 8 + 8, :].T
        cum_s = aux[16 + b * 8 : 16 + b * 8 + 8, :]
        for pair in range(heads // 2):
            cols = slice(pair * 128, (pair + 1) * 128)
            xf = x_ref[at, cols].astype(F32)
            parts = []
            for h in (2 * pair, 2 * pair + 1):
                gap = jnp.where(mask, cum_t[:, h : h + 1] - cum_s[h : h + 1, :], -1e30)
                parts.append((jnp.exp2(gap) * scores).astype(BF16))
            stacked = jnp.concatenate(
                [
                    jnp.where(left, xf, 0.0).astype(BF16),
                    jnp.where(left, 0.0, xf).astype(BF16),
                ],
                axis=0,
            )
            mixed = jnp.dot(
                jnp.concatenate(parts, axis=1), stacked, preferred_element_type=F32
            )
            y_ref[at, cols] = (mixed + skip_ref[0:1, cols] * xf).astype(BF16)


def rounds_of(count):
    rounds, window = [], 1
    while 4 * window < count - 1:
        rounds.append([window * k for k in (1, 2, 3)])
        window *= 4
    rounds.append([1 + window * k for k in range(-(-(count - 1) // window))])
    return rounds


def exchange_kernel(count, nc, heads, pieces, *refs):
    sm, skip = refs[:2]
    halves = (refs[2:12], refs[12:22])
    mixed = (refs[22:24], refs[24:26])
    into_f, into_r = refs[26:28]
    sent, landed, held, fade, send_sem, recv_sem = refs[28:]
    (st_f0, st_r0, dec_f0, dec_r0), (st_f1, st_r1, dec_f1, dec_r1) = (h[:4] for h in halves)
    index = lax.axis_index("ctx")
    rounds = rounds_of(count)
    signs = (1, -1)

    def reaches(step):
        return index + step < count if step > 0 else index + step >= 0

    def peer(step):
        return {"ctx": index + step}

    barrier = pltpu.get_barrier_semaphore()
    steps = sorted({sign * s for r in rounds for s in r for sign in signs})
    for step in steps:

        @pl.when(reaches(step))
        def _(step=step):
            pl.semaphore_signal(
                barrier, inc=1, device_id=peer(step), device_id_type=pl.DeviceIdType.MESH
            )

    peers = sum(
        1 - lax.div(index + step, count) if step > 0 else lax.div(index + step + count, count)
        for step in steps
    )
    pl.semaphore_wait(barrier, peers)

    held[0] = st_f0[...] * dec_f1[0:1, :] + st_f1[...]
    held[1] = st_r1[...] * dec_r0[0:1, :] + st_r0[...]
    fade[0] = dec_f0[...] * dec_f1[...]
    fade[1] = dec_r0[...] * dec_r1[...]
    jobs = (True, False)
    slot = 0
    for number, shifts in enumerate(rounds):
        last = number == len(rounds) - 1
        copies = []
        for stream, sign in enumerate(signs):
            at = number * 2 + stream
            decay = fade[stream]
            high = decay.astype(BF16)
            low = (decay - high.astype(F32)).astype(BF16)
            sent[at, 0:NSTATE, :] = held[stream].astype(BF16)
            sent[at, NSTATE : NSTATE + 16, :] = jnp.concatenate([high, low], axis=0)
            for s in shifts:
                copy = pltpu.make_async_remote_copy(
                    src_ref=sent.at[at],
                    dst_ref=landed.at[slot],
                    send_sem=send_sem.at[slot],
                    recv_sem=recv_sem.at[slot],
                    device_id=peer(sign * s),
                    device_id_type=pl.DeviceIdType.MESH,
                )
                copies.append((stream, sign * s, slot, copy))
                slot += 1

                @pl.when(reaches(sign * s))
                def _(copy=copy):
                    copy.start()

        if number < len(jobs):
            forward = jobs[number]
            for half in (0, 1):
                x_ref, bc_ref, aux_ref = halves[half][4:7] if forward else halves[half][7:10]
                y_ref = mixed[half][number]

                def body(chunk, carry):
                    intra_rows(
                        forward, heads, pieces, sm, x_ref, bc_ref, aux_ref, skip, y_ref,
                        half * nc * CHUNK, chunk,
                    )
                    return carry

                lax.fori_loop(0, nc, body, 0)

        if last:
            held[...] = jnp.zeros_like(held)
            fade[...] = jnp.ones_like(fade)
        for stream, step, at, copy in copies:

            @pl.when(reaches(-step))
            def _(stream=stream, at=at, copy=copy):
                copy.wait_recv()
                more = landed[at, 0:NSTATE, :].astype(F32)
                tail = landed[at, NSTATE : NSTATE + 16, :].astype(F32)
                held[stream] = held[stream] + fade[stream, 0:1, :] * more
                fade[stream] = fade[stream] * (tail[0:8] + tail[8:16])

        for stream, step, at, copy in copies:

            @pl.when(reaches(step))
            def _(copy=copy):
                copy.wait_send()

    into_f[0] = held[0]
    into_f[1] = st_f0[...] + dec_f0[0:1, :] * held[0]
    into_r[0] = st_r1[...] + dec_r1[0:1, :] * held[1]
    into_r[1] = held[1]


def finish_kernel(nc, inner, *refs):
    ins, par = refs[0:12], refs[12:15]
    outs = refs[15:19]
    grown = refs[19:21]
    gain_ref, e1, e2 = par
    step = pl.program_id(0)

    @pl.when(step == 0)
    def _():
        grown[0][...] = jnp.ones_like(grown[0])
        grown[1][...] = jnp.ones_like(grown[1])

    ones = jnp.ones((8, inner), BF16)
    for stream in (0, 1):
        y_ref, z_ref, bc_ref, aux_ref, before_ref, into_ref = ins[stream * 6 : stream * 6 + 6]
        g_out, ss_out = outs[stream * 2 : stream * 2 + 2]
        into = into_ref[...]
        for b in (0, 1) if stream == 0 else (1, 0):
            at = slice(b * SUB, (b + 1) * SUB)
            grow = grown[stream][...]
            state = (before_ref[b].astype(F32) + grow * into).astype(BF16)
            factor = expand_rows(aux_ref[0, 32 + b * 8 : 40 + b * 8, :], e2[...])
            inter = jnp.dot(bc_ref[at, NSTATE:], state, preferred_element_type=F32)
            mixed = y_ref[at, :].astype(F32) + inter * factor
            gated = mixed * silu(z_ref[at, :].astype(F32))
            ss_out[:, at] = lax.dot_general(
                ones, (gated * gated).astype(BF16), NT, preferred_element_type=F32
            )
            g_out[at, :] = (gated * gain_ref[0:1, :]).astype(BF16)
            whole = aux_ref[0, 48 + b * 8 : 56 + b * 8, 0:1]
            grown[stream][...] = grow * jnp.sum(whole * e1[...], axis=0, keepdims=True)


def output_kernel(mp, total_width, ss_ref, gf_ref, gr_ref, wf_ref, wr_ref, *outs):
    factor = lax.rsqrt(ss_ref[...] * (1.0 / total_width) + EPSILON).T
    width = wf_ref.shape[1] // mp
    for k in range(mp):
        cols = slice(k * width, (k + 1) * width)
        part = factor[:, 0:1] * jnp.dot(gf_ref[...], wf_ref[:, cols], preferred_element_type=F32)
        part = part + factor[:, 4:5] * jnp.dot(
            gr_ref[...], wr_ref[:, cols], preferred_element_type=F32
        )
        outs[k][...] = part.astype(outs[k].dtype)


def shift(value, axis, by, wrap):
    count = lax.axis_size(axis)
    if wrap:
        pairs = [(i, (i + by) % count) for i in range(count)]
    else:
        pairs = [(i, i + by) for i in range(count) if 0 <= i + by < count]
    return lax.ppermute(value, axis, pairs)


def cost(flops, size, trans=0):
    return pl.CostEstimate(flops=flops, bytes_accessed=size, transcendentals=trans)


def shards(
    hidden, w_x, w_z, w_bc, w_dt, conv_x, conv_bc, dt_bias, decay_rate, skip_gain, norm_gain,
    w_out, piece_lengths,
):
    mp = lax.axis_size("mp")
    me = lax.axis_index("mp")
    rows, width = hidden.shape
    model = width * mp
    heads = dt_bias.shape[0]
    inner = heads * HEAD_DIM
    mixing = inner + 2 * NSTATE
    pieces = piece_lengths.shape[0]
    part_rows = rows // 2
    nc = part_rows // CHUNK
    params = pltpu.CompilerParams(vmem_limit_bytes=VMEM_LIMIT)

    from_below = shift(hidden[rows - 16 :], "ctx", 1, False)
    from_above = shift(hidden[:16], "ctx", -1, False)
    halo_own = jnp.concatenate(
        [
            from_below,
            hidden[part_rows : part_rows + 16],
            hidden[part_rows - 16 : part_rows],
            from_above,
        ],
        axis=0,
    )
    halos = [halo_own] + [shift(halo_own, "mp", k, True) for k in range(1, mp)]
    lower, upper = hidden[:part_rows], hidden[part_rows:]
    low_blocks = [shift(lower, "mp", k, True) for k in range(1, mp)]
    upper, *low_blocks = lax.optimization_barrier((upper, *low_blocks))
    high_blocks = [shift(upper, "mp", k, True) for k in range(1, mp)]
    blocks = ([lower] + low_blocks, [upper] + high_blocks)

    place = jnp.arange(model, dtype=jnp.int32)
    came = lax.rem(me - place // width + mp, mp) * width + lax.rem(place, width)
    columns = jnp.arange(model, dtype=jnp.int32)[None, :]
    pick_f = (came[:, None] == columns).astype(BF16)
    pick_r = (model - 1 - came[:, None] == columns).astype(BF16)
    w_in = jnp.concatenate([w_x, w_bc, w_z], axis=1)
    w_f = jnp.dot(pick_f, w_in, preferred_element_type=F32).astype(BF16)
    w_r = jnp.dot(pick_r, w_in, preferred_element_type=F32).astype(BF16)
    pad = 8 - heads
    dt_pad = jnp.pad(w_dt, ((0, 0), (0, pad)))
    dt_t = lax.dot_general(
        dt_pad,
        jnp.concatenate([pick_f, pick_r], axis=0),
        (((0,), (1,)), ((), ())),
        preferred_element_type=F32,
    ).astype(BF16)
    w_dt2 = jnp.concatenate([dt_t[:, :model], dt_t[:, model:]], axis=0)
    goes = lax.rem(me + place // width, mp) * width + lax.rem(place, width)
    out_f = jnp.dot(
        w_out, (columns.T == goes[None, :]).astype(BF16), preferred_element_type=F32
    ).astype(BF16)
    out_r = jnp.dot(
        w_out, (columns.T == model - 1 - goes[None, :]).astype(BF16), preferred_element_type=F32
    ).astype(BF16)

    bounds = jnp.cumsum(piece_lengths).astype(jnp.int32)
    first_row = (lax.axis_index("ctx") * rows).astype(jnp.int32)[None]
    sms = [jnp.concatenate([bounds, first_row + half * part_rows]) for half in (0, 1)]
    conv_w = jnp.pad(jnp.concatenate([conv_x, conv_bc], axis=1), ((0, 4), (0, 0)))
    bias = jnp.pad(dt_bias, (0, pad))
    rate = jnp.pad(-LOG2E * decay_rate, (0, pad))
    head_par = jnp.broadcast_to(
        jnp.concatenate([bias, bias, rate, rate])[:, None], (32, SUB)
    ).astype(F32)
    owner = jnp.arange(inner, dtype=jnp.int32)[None, :] // HEAD_DIM
    e1 = (jnp.arange(8, dtype=jnp.int32)[:, None] == owner).astype(F32)
    e2 = jnp.concatenate([e1, e1], axis=0).astype(BF16)
    skip8 = jnp.broadcast_to(jnp.repeat(skip_gain, HEAD_DIM)[None, :], (8, inner))
    gain8 = jnp.broadcast_to(norm_gain[None, :], (8, inner))

    smem = pl.BlockSpec(memory_space=pltpu.SMEM)

    def whole(shape):
        return pl.BlockSpec(shape, lambda i: (0,) * len(shape))

    def up(cols):
        return pl.BlockSpec((CHUNK, cols), lambda i: (i, 0))

    def down(cols):
        return pl.BlockSpec((CHUNK, cols), lambda i: (nc - 1 - i, 0))

    aux_up = pl.BlockSpec((1, 64, SUB), lambda i: (i, 0, 0))
    aux_down = pl.BlockSpec((1, 64, SUB), lambda i: (nc - 1 - i, 0, 0))
    st_up = pl.BlockSpec((2, NSTATE, inner), lambda i: (i, 0, 0))
    st_down = pl.BlockSpec((2, NSTATE, inner), lambda i: (nc - 1 - i, 0, 0))

    def sds(shape, dtype):
        return jax.ShapeDtypeStruct(shape, dtype)

    stream_shapes = [
        sds((part_rows, inner), BF16),
        sds((part_rows, 2 * NSTATE), BF16),
        sds((part_rows, inner), BF16),
        sds((nc, 64, SUB), F32),
        sds((2 * nc, NSTATE, inner), BF16),
    ]
    project = pl.pallas_call(
        functools.partial(project_kernel, nc, mp, inner, pieces),
        grid=(nc,),
        in_specs=[smem]
        + [up(width)] * mp
        + [down(width)] * mp
        + [whole((32, width))] * mp
        + [
            whole((model, mixing + inner)),
            whole((model, mixing + inner)),
            whole((16, model)),
            whole((8, mixing)),
            whole((32, SUB)),
            whole((8, inner)),
            whole((16, inner)),
        ],
        out_specs=[up(inner), up(2 * NSTATE), up(inner), aux_up, st_up]
        + [down(inner), down(2 * NSTATE), down(inner), aux_down, st_down]
        + [whole((NSTATE, inner))] * 2
        + [whole((8, inner))] * 2,
        out_shape=stream_shapes
        + stream_shapes
        + [sds((NSTATE, inner), F32)] * 2
        + [sds((8, inner), F32)] * 2,
        scratch_shapes=[
            pltpu.VMEM((CHUNK + 8, mixing), F32),
            pltpu.VMEM((CHUNK + 8, mixing), F32),
            pltpu.VMEM((NSTATE, inner), F32),
            pltpu.VMEM((NSTATE, inner), F32),
            pltpu.VMEM((8, inner), F32),
            pltpu.VMEM((8, inner), F32),
        ],
        compiler_params=params,
        cost_estimate=cost(4 * part_rows * model * (mixing + inner), 10 << 20),
        name="project",
    )
    made = [
        project(
            sms[half], *blocks[half], *blocks[half],
            *[h[half * 32 : half * 32 + 32] for h in halos],
            w_f, w_r, w_dt2, conv_w, head_par, e1, e2,
        )
        for half in (0, 1)
    ]

    count = lax.axis_size("ctx")
    rounds = rounds_of(count)
    slots = 2 * sum(len(r) for r in rounds)
    packed = NSTATE + 16
    vmem = pl.BlockSpec(memory_space=pltpu.VMEM)
    *mixed, into_f, into_r = pl.pallas_call(
        functools.partial(exchange_kernel, count, nc, heads, pieces),
        in_specs=[smem] + [vmem] * 21,
        out_specs=[vmem] * 6,
        out_shape=[sds((part_rows, inner), BF16)] * 4 + [sds((2, NSTATE, inner), F32)] * 2,
        scratch_shapes=[
            pltpu.VMEM((2 * len(rounds), packed, inner), BF16),
            pltpu.VMEM((slots, packed, inner), BF16),
            pltpu.VMEM((2, NSTATE, inner), F32),
            pltpu.VMEM((2, 8, inner), F32),
            pltpu.SemaphoreType.DMA((slots,)),
            pltpu.SemaphoreType.DMA((slots,)),
        ],
        compiler_params=pltpu.CompilerParams(
            vmem_limit_bytes=VMEM_LIMIT, collective_id=0, has_side_effects=True
        ),
        cost_estimate=cost(40 * rows * SUB * inner, 16 << 20, 2 * rows * SUB * heads),
        name="exchange",
    )(
        sms[0],
        skip8,
        *[
            value
            for m in made
            for value in (*m[10:14], m[0], m[1], m[3], m[5], m[6], m[8])
        ],
    )

    finish = pl.pallas_call(
        functools.partial(finish_kernel, nc, inner),
        grid=(nc,),
        in_specs=[up(inner), up(inner), up(2 * NSTATE), aux_up, st_up, whole((NSTATE, inner))]
        + [down(inner), down(inner), down(2 * NSTATE), aux_down, st_down, whole((NSTATE, inner))]
        + [whole((8, inner)), whole((8, inner)), whole((16, inner))],
        out_specs=[
            up(inner),
            pl.BlockSpec((8, CHUNK), lambda i: (0, i)),
            down(inner),
            pl.BlockSpec((8, CHUNK), lambda i: (0, nc - 1 - i)),
        ],
        out_shape=[sds((part_rows, inner), BF16), sds((8, part_rows), F32)] * 2,
        scratch_shapes=[pltpu.VMEM((1, inner), F32)] * 2,
        compiler_params=params,
        cost_estimate=cost(4 * part_rows * NSTATE * inner, 12 << 20),
        name="finish",
    )
    output = pl.pallas_call(
        functools.partial(output_kernel, mp, inner * mp),
        grid=(nc,),
        in_specs=[
            pl.BlockSpec((8, CHUNK), lambda i: (0, i)),
            up(inner),
            up(inner),
            whole((inner, model)),
            whole((inner, model)),
        ],
        out_specs=[up(width)] * mp,
        out_shape=[sds((part_rows, width), F32)] + [sds((part_rows, width), BF16)] * (mp - 1),
        compiler_params=params,
        cost_estimate=cost(4 * part_rows * inner * model, 4 << 20),
        name="output",
    )
    forward_rows = jnp.arange(8, dtype=jnp.int32)[:, None] < 4
    gated, squares = [], []
    for half, m in enumerate(made):
        gated_f, square_f, gated_r, square_r = finish(
            mixed[2 * half], m[2], m[1], m[3], m[4], into_f[half],
            mixed[2 * half + 1], m[7], m[6], m[8], m[9], into_r[half],
            gain8, e1, e2,
        )
        gated.append((gated_f, gated_r))
        squares.append(jnp.where(forward_rows, square_f, square_r))
    other = [[shift(sq, "mp", k, True) for k in range(1, mp)] for sq in squares]
    totals = [sum(got, sq) for got, sq in zip(other, squares)]
    first = output(totals[0], *gated[0], out_f, out_r)
    first, totals[1] = lax.optimization_barrier((first, totals[1]))
    results = []
    for parts in (first, output(totals[1], *gated[1], out_f, out_r)):
        result = parts[0]
        for k in range(1, mp):
            result = result + shift(parts[k], "mp", k, True).astype(F32)
        results.append(result.astype(BF16))
    return jnp.concatenate(results, axis=0)


def solution(mesh):
    return jax.shard_map(
        shards,
        mesh=mesh,
        in_specs=(
            P("ctx", "mp"), P(None, "mp"), P(None, "mp"), P(), P(None, "mp"), P(None, "mp"), P(),
            P("mp"), P("mp"), P("mp"), P("mp"), P("mp", None), P(),
        ),
        out_specs=P("ctx", "mp"),
        check_vma=False,
    )
```

```python
import functools
import jax
import jax.numpy as jnp
from jax import lax
from jax.experimental import pallas as pl
from jax.experimental.pallas import tpu as pltpu
from jax.sharding import PartitionSpec as P

HEAD_DIM = 64
NSTATE = 128
SUB = 128
CHUNK = 256
EPSILON = 1e-05
LOG2E = 1.4426950408889634
F32 = jnp.float32
BF16 = jnp.bfloat16
BIG = 1 << 30
VMEM_LIMIT = 48 * 1024 * 1024

NT = (((1,), (1,)), ((), ()))
TN = (((0,), (0,)), ((), ()))


def piece_start(sm, pieces, pos):
    out = jnp.zeros_like(pos)
    for k in range(pieces):
        bound = sm[k]
        out = jnp.maximum(out, jnp.where(pos >= bound, bound, 0))
    return out


def piece_end(sm, pieces, pos):
    out = jnp.full_like(pos, BIG)
    for k in range(pieces):
        bound = sm[k]
        out = jnp.minimum(out, jnp.where(pos < bound, bound, BIG))
    return out


def silu(value):
    half = 0.5 * value
    return half * jnp.tanh(half) + half


def expand_rows(weights, expander2):
    high = weights.astype(BF16)
    low = (weights - high.astype(F32)).astype(BF16)
    both = jnp.concatenate([high, low], axis=0)
    return lax.dot_general(both, expander2, TN, preferred_element_type=F32)


def project_kernel(nc, mp, inner, pieces, *refs):
    sm = refs[0]
    hf, hr, halo = refs[1 : 1 + mp], refs[1 + mp : 1 + 2 * mp], refs[1 + 2 * mp : 1 + 3 * mp]
    (wf, wr, wdt, cw, head_par, e1, e2) = refs[1 + 3 * mp : 8 + 3 * mp]
    outs = refs[8 + 3 * mp : 22 + 3 * mp]
    buf_f, buf_r, st_f, st_r, dec_f, dec_r = refs[22 + 3 * mp :]
    step = pl.program_id(0)
    base = sm[pieces]
    mixing = inner + 2 * NSTATE
    width = wf.shape[0] // mp

    def dots(blocks, weight, columns):
        total = None
        for b in range(mp):
            part = jnp.dot(
                blocks[b], weight[b * width : (b + 1) * width, columns], preferred_element_type=F32
            )
            total = part if total is None else total + part
        return total

    @pl.when(step == 0)
    def _():
        low = dots([h[0:16, :] for h in halo], wf, slice(0, mixing))
        high = dots([h[16:32, :] for h in halo], wr, slice(0, mixing))
        buf_f[0:8, :] = low[8:16].astype(BF16).astype(F32)
        buf_r[CHUNK : CHUNK + 8, :] = high[0:8].astype(BF16).astype(F32)
        st_f[...] = jnp.zeros_like(st_f)
        st_r[...] = jnp.zeros_like(st_r)
        dec_f[...] = jnp.ones_like(dec_f)
        dec_r[...] = jnp.ones_like(dec_r)

    @pl.when(step > 0)
    def _():
        buf_f[0:8, :] = buf_f[CHUNK : CHUNK + 8, :]
        buf_r[CHUNK : CHUNK + 8, :] = buf_r[0:8, :]

    rows = lax.broadcasted_iota(jnp.int32, (SUB, SUB), 0)
    lanes = lax.broadcasted_iota(jnp.int32, (SUB, SUB), 1)
    for forward in (True, False):
        blocks = [h[...] for h in (hf if forward else hr)]
        weight = wf if forward else wr
        buf = buf_f if forward else buf_r
        state, decay = (st_f, dec_f) if forward else (st_r, dec_r)
        x_out, bc_out, z_out, aux_out, before_out = outs[:5] if forward else outs[5:10]
        chunk = step if forward else nc - 1 - step
        first = base + chunk * CHUNK
        own = 8 if forward else 0
        buf[own : own + CHUNK, :] = (
            dots(blocks, weight, slice(0, mixing)).astype(BF16).astype(F32)
        )
        z_out[...] = dots(blocks, weight, slice(mixing, mixing + inner)).astype(BF16)

        raw = None
        lo = 0 if forward else 8
        for b in range(mp):
            part = lax.dot_general(
                wdt[lo : lo + 8, b * width : (b + 1) * width],
                blocks[b],
                NT,
                preferred_element_type=F32,
            )
            raw = part if raw is None else raw + part
        raw = raw.astype(BF16).astype(F32)
        raw = jnp.concatenate([raw[:, :SUB], raw[:, SUB:]], axis=0)
        par = head_par[...]
        shifted = raw + par[0:16]
        step_dt = jnp.maximum(shifted, 0.0) + jnp.log1p(jnp.exp(-jnp.abs(shifted)))
        log_decay = step_dt * par[16:32]
        tri = jnp.where(rows <= lanes if forward else rows >= lanes, 1.0, 0.0).astype(F32)
        cum = jnp.dot(
            log_decay, tri, precision=lax.Precision.HIGHEST, preferred_element_type=F32
        )
        total = cum[:, SUB - 1 : SUB] if forward else cum[:, 0:1]
        block_first = first + SUB * (lax.broadcasted_iota(jnp.int32, (16, SUB), 0) // 8)
        position = block_first + lax.broadcasted_iota(jnp.int32, (16, SUB), 1)
        start = piece_start(sm, pieces, position)
        end = piece_end(sm, pieces, position)
        block_last = block_first + SUB - 1
        if forward:
            to_end_ok = end > block_last
            from_start_ok = start < block_first
            whole_ok = piece_start(sm, pieces, block_last) < block_first
        else:
            to_end_ok = start <= block_first
            from_start_ok = end > block_last + 1
            whole_ok = piece_end(sm, pieces, block_first) > block_last + 1
        to_end = jnp.where(to_end_ok, jnp.exp2(total - cum) * step_dt, 0.0)
        from_start = jnp.where(from_start_ok, jnp.exp2(cum), 0.0)
        whole = jnp.where(whole_ok, jnp.exp2(jnp.broadcast_to(total, cum.shape)), 0.0)
        aux_out[0, 0:16, :] = cum
        aux_out[0, 16:32, :] = cum - jnp.log2(step_dt)
        aux_out[0, 32:48, :] = from_start
        aux_out[0, 48:64, :] = whole

        for b in (0, 1) if forward else (1, 0):
            at = first + b * SUB + rows
            if forward:
                room = at - piece_start(sm, pieces, at)
            else:
                room = piece_end(sm, pieces, at) - 1 - at
            same = [None] + [room >= j for j in (1, 2, 3)]
            r0 = own + b * SUB
            out_rows = slice(b * SUB, (b + 1) * SUB)
            for g in range(mixing // 128):
                cols = slice(g * 128, (g + 1) * 128)
                acc = buf[r0 : r0 + SUB, cols] * cw[3:4, cols]
                for j in (1, 2, 3):
                    off = r0 - j if forward else r0 + j
                    tap = buf[off : off + SUB, cols] * cw[3 - j : 4 - j, cols]
                    acc = acc + jnp.where(same[j], tap, 0.0)
                value = silu(acc).astype(BF16)
                if g * 128 < inner:
                    x_out[out_rows, cols] = value
                else:
                    bc_out[out_rows, slice(g * 128 - inner, g * 128 - inner + 128)] = value
            hb = slice(b * 8, b * 8 + 8)
            weights = expand_rows(to_end[hb], e2[...])
            scaled = (x_out[out_rows, :].astype(F32) * weights).astype(BF16)
            added = lax.dot_general(
                bc_out[out_rows, 0:NSTATE], scaled, TN, preferred_element_type=F32
            )
            grow = jnp.sum(whole[hb, 0:1] * e1[...], axis=0, keepdims=True)
            held = state[...]
            before_out[b] = held.astype(BF16)
            state[...] = held * grow + added
            decay[...] = decay[...] * grow

    outs[10][...] = st_f[...]
    outs[11][...] = st_r[...]
    outs[12][...] = dec_f[...]
    outs[13][...] = dec_r[...]


def intra_rows(forward, heads, pieces, sm, x_ref, bc_ref, aux_ref, skip_ref, y_ref, offset, chunk):
    base = sm[pieces] + offset
    rows = lax.broadcasted_iota(jnp.int32, (SUB, SUB), 0)
    lanes = lax.broadcasted_iota(jnp.int32, (SUB, SUB), 1)
    left = lanes < HEAD_DIM
    aux = aux_ref[chunk]
    for b in (0, 1):
        at = pl.ds(pl.multiple_of(chunk * CHUNK + b * SUB, SUB), SUB)
        begin = base + chunk * CHUNK + b * SUB
        if forward:
            mask = (lanes <= rows) & (begin + lanes >= piece_start(sm, pieces, begin + rows))
        else:
            mask = (lanes >= rows) & (begin + lanes < piece_end(sm, pieces, begin + rows))
        scores = lax.dot_general(
            bc_ref[at, NSTATE:], bc_ref[at, 0:NSTATE], NT, preferred_element_type=F32
        )
        cum_t = aux[b * 8 : b * 8 + 8, :].T
        cum_s = aux[16 + b * 8 : 16 + b * 8 + 8, :]
        for pair in range(heads // 2):
            cols = slice(pair * 128, (pair + 1) * 128)
            xf = x_ref[at, cols].astype(F32)
            parts = []
            for h in (2 * pair, 2 * pair + 1):
                gap = jnp.where(mask, cum_t[:, h : h + 1] - cum_s[h : h + 1, :], -1e30)
                parts.append((jnp.exp2(gap) * scores).astype(BF16))
            stacked = jnp.concatenate(
                [
                    jnp.where(left, xf, 0.0).astype(BF16),
                    jnp.where(left, 0.0, xf).astype(BF16),
                ],
                axis=0,
            )
            mixed = jnp.dot(
                jnp.concatenate(parts, axis=1), stacked, preferred_element_type=F32
            )
            y_ref[at, cols] = (mixed + skip_ref[0:1, cols] * xf).astype(BF16)


def rounds_of(count):
    rounds, window = [], 1
    while 4 * window < count - 1:
        rounds.append([window * k for k in (1, 2, 3)])
        window *= 4
    rounds.append([1 + window * k for k in range(-(-(count - 1) // window))])
    return rounds


def exchange_kernel(count, nc, heads, pieces, *refs):
    sm, skip = refs[:2]
    halves = (refs[2:12], refs[12:22])
    mixed = (refs[22:24], refs[24:26])
    into_f, into_r = refs[26:28]
    own, own_fade, held, fade, full = refs[28:33]
    pair_sent, pair_landed, sent, landed, last_sent, last_landed = refs[33:39]
    pair_sems, send_sem, recv_sem, last_sems = refs[39:]
    (st_f0, st_r0, dec_f0, dec_r0), (st_f1, st_r1, dec_f1, dec_r1) = (h[:4] for h in halves)
    index = lax.axis_index("ctx")
    core = lax.rem(index, 2)
    sibling = {"ctx": index + 1 - 2 * core}
    rounds = rounds_of(count // 2)
    signs = (1, -1)
    part = NSTATE // 2
    mine = pl.ds(pl.multiple_of(core * part, part), part)
    theirs = pl.ds(pl.multiple_of((1 - core) * part, part), part)

    def reaches(step):
        return index + step < count if step > 0 else index + step >= 0

    def send(src, dst, send_at, recv_at, target):
        return pltpu.make_async_remote_copy(
            src_ref=src,
            dst_ref=dst,
            send_sem=send_at,
            recv_sem=recv_at,
            device_id=target,
            device_id_type=pl.DeviceIdType.MESH,
        )

    def signal(target):
        pl.semaphore_signal(barrier, inc=1, device_id=target, device_id_type=pl.DeviceIdType.MESH)

    def pack_decay(decay):
        high = decay.astype(BF16)
        return jnp.concatenate([high, (decay - high.astype(F32)).astype(BF16)], axis=0)

    def on_first(shape, yes, no):
        return jnp.where(jnp.full(shape, core, jnp.int32) == 0, yes, no)

    work = [(stream, half) for stream in (0, 1) for half in (0, 1)]

    def compute(pieces_now):
        for stream, half in pieces_now:
            x_ref, bc_ref, aux_ref = halves[half][4 + 3 * stream : 7 + 3 * stream]
            y_ref = mixed[half][stream]

            def body(chunk, carry):
                intra_rows(
                    stream == 0, heads, pieces, sm, x_ref, bc_ref, aux_ref, skip, y_ref,
                    half * nc * CHUNK, chunk,
                )
                return carry

            lax.fori_loop(0, nc, body, 0)

    barrier = pltpu.get_barrier_semaphore()
    steps = sorted({2 * sign * s for r in rounds for s in r for sign in signs})
    signal(sibling)
    for step in steps:

        @pl.when(reaches(step))
        def _(step=step):
            signal({"ctx": index + step})

    peers = 1 + sum(
        1 - lax.div(index + step, count) if step > 0 else lax.div(index + step + count, count)
        for step in steps
    )
    pl.semaphore_wait(barrier, peers)

    own[0] = st_f0[...] * dec_f1[0:1, :] + st_f1[...]
    own[1] = st_r1[...] * dec_r0[0:1, :] + st_r0[...]
    own_fade[0] = dec_f0[...] * dec_f1[...]
    own_fade[1] = dec_r0[...] * dec_r1[...]
    swaps = []
    for stream in (0, 1):
        pair_sent[stream, 0:NSTATE, :] = own[stream].astype(BF16)
        pair_sent[stream, NSTATE : NSTATE + 16, :] = pack_decay(own_fade[stream])
        swap = send(
            pair_sent.at[stream], pair_landed.at[stream],
            pair_sems.at[stream], pair_sems.at[2 + stream], sibling,
        )
        swap.start()
        swaps.append(swap)
    compute(work[0:1])
    for swap in swaps:
        swap.wait()
    shape = held.shape[1:]
    for stream in (0, 1):
        tail = pair_landed[stream, NSTATE : NSTATE + 16, :].astype(F32)
        other_fade = tail[0:8] + tail[8:16]
        other = pair_landed[stream, mine, :].astype(F32)
        here = own[stream, mine, :]
        before = other_fade[0:1] * here + other
        after = own_fade[stream, 0:1, :] * other + here
        held[stream] = on_first(shape, *((before, after) if stream == 0 else (after, before)))
        fade[stream] = own_fade[stream] * other_fade

    slot = 0
    for number, shifts in enumerate(rounds):
        last = number == len(rounds) - 1
        copies = []
        for stream, sign in enumerate(signs):
            at = number * 2 + stream
            sent[at, 0:part, :] = held[stream].astype(BF16)
            sent[at, part : part + 16, :] = pack_decay(fade[stream])
            for s in shifts:
                step = 2 * sign * s
                copy = send(
                    sent.at[at], landed.at[slot],
                    send_sem.at[slot], recv_sem.at[slot], {"ctx": index + step},
                )
                copies.append((stream, step, slot, copy))
                slot += 1

                @pl.when(reaches(step))
                def _(copy=copy):
                    copy.start()

        if len(rounds) == 1:
            compute(work[1:])
        elif number == 0:
            compute(work[1:3])
        elif number == 1:
            compute(work[3:])
        if last:
            held[...] = jnp.zeros_like(held)
            fade[...] = jnp.ones_like(fade)
        for stream, step, at, copy in copies:

            @pl.when(reaches(-step))
            def _(stream=stream, at=at, copy=copy):
                copy.wait_recv()
                more = landed[at, 0:part, :].astype(F32)
                tail = landed[at, part : part + 16, :].astype(F32)
                held[stream] = held[stream] + fade[stream, 0:1, :] * more
                fade[stream] = fade[stream] * (tail[0:8] + tail[8:16])

        for stream, step, at, copy in copies:

            @pl.when(reaches(step))
            def _(copy=copy):
                copy.wait_send()

    swaps = []
    for stream in (0, 1):
        last_sent[stream] = held[stream].astype(BF16)
        swap = send(
            last_sent.at[stream], last_landed.at[stream],
            last_sems.at[stream], last_sems.at[2 + stream], sibling,
        )
        swap.start()
        swaps.append(swap)
    for stream in (0, 1):
        swaps[stream].wait()
        full[stream, mine, :] = held[stream]
        full[stream, theirs, :] = last_landed[stream].astype(F32)
        tail = pair_landed[stream, NSTATE : NSTATE + 16, :].astype(F32)
        outer = full[stream]
        passed = (tail[0:1] + tail[8:9]) * outer + pair_landed[stream, 0:NSTATE, :].astype(F32)
        into = on_first(
            outer.shape, *((outer, passed) if stream == 0 else (passed, outer))
        )
        if stream == 0:
            into_f[0] = into
            into_f[1] = st_f0[...] + dec_f0[0:1, :] * into
        else:
            into_r[0] = st_r1[...] + dec_r1[0:1, :] * into
            into_r[1] = into


def finish_kernel(nc, inner, *refs):
    ins, par = refs[0:12], refs[12:15]
    outs = refs[15:19]
    grown = refs[19:21]
    gain_ref, e1, e2 = par
    step = pl.program_id(0)

    @pl.when(step == 0)
    def _():
        grown[0][...] = jnp.ones_like(grown[0])
        grown[1][...] = jnp.ones_like(grown[1])

    ones = jnp.ones((8, inner), BF16)
    for stream in (0, 1):
        y_ref, z_ref, bc_ref, aux_ref, before_ref, into_ref = ins[stream * 6 : stream * 6 + 6]
        g_out, ss_out = outs[stream * 2 : stream * 2 + 2]
        into = into_ref[...]
        for b in (0, 1) if stream == 0 else (1, 0):
            at = slice(b * SUB, (b + 1) * SUB)
            grow = grown[stream][...]
            state = (before_ref[b].astype(F32) + grow * into).astype(BF16)
            factor = expand_rows(aux_ref[0, 32 + b * 8 : 40 + b * 8, :], e2[...])
            inter = jnp.dot(bc_ref[at, NSTATE:], state, preferred_element_type=F32)
            mixed = y_ref[at, :].astype(F32) + inter * factor
            gated = mixed * silu(z_ref[at, :].astype(F32))
            ss_out[:, at] = lax.dot_general(
                ones, (gated * gated).astype(BF16), NT, preferred_element_type=F32
            )
            g_out[at, :] = (gated * gain_ref[0:1, :]).astype(BF16)
            whole = aux_ref[0, 48 + b * 8 : 56 + b * 8, 0:1]
            grown[stream][...] = grow * jnp.sum(whole * e1[...], axis=0, keepdims=True)


def output_kernel(mp, total_width, ss_ref, gf_ref, gr_ref, wf_ref, wr_ref, *outs):
    factor = lax.rsqrt(ss_ref[...] * (1.0 / total_width) + EPSILON).T
    width = wf_ref.shape[1] // mp
    for k in range(mp):
        cols = slice(k * width, (k + 1) * width)
        part = factor[:, 0:1] * jnp.dot(gf_ref[...], wf_ref[:, cols], preferred_element_type=F32)
        part = part + factor[:, 4:5] * jnp.dot(
            gr_ref[...], wr_ref[:, cols], preferred_element_type=F32
        )
        outs[k][...] = part.astype(outs[k].dtype)


def shift(value, axis, by, wrap):
    count = lax.axis_size(axis)
    if wrap:
        pairs = [(i, (i + by) % count) for i in range(count)]
    else:
        pairs = [(i, i + by) for i in range(count) if 0 <= i + by < count]
    return lax.ppermute(value, axis, pairs)


def cost(flops, size, trans=0):
    return pl.CostEstimate(flops=flops, bytes_accessed=size, transcendentals=trans)


def shards(
    hidden, w_x, w_z, w_bc, w_dt, conv_x, conv_bc, dt_bias, decay_rate, skip_gain, norm_gain,
    w_out, piece_lengths,
):
    mp = lax.axis_size("mp")
    me = lax.axis_index("mp")
    rows, width = hidden.shape
    model = width * mp
    heads = dt_bias.shape[0]
    inner = heads * HEAD_DIM
    mixing = inner + 2 * NSTATE
    pieces = piece_lengths.shape[0]
    part_rows = rows // 2
    nc = part_rows // CHUNK
    params = pltpu.CompilerParams(vmem_limit_bytes=VMEM_LIMIT)

    from_below = shift(hidden[rows - 16 :], "ctx", 1, False)
    from_above = shift(hidden[:16], "ctx", -1, False)
    halo_own = jnp.concatenate(
        [
            from_below,
            hidden[part_rows : part_rows + 16],
            hidden[part_rows - 16 : part_rows],
            from_above,
        ],
        axis=0,
    )
    halos = [halo_own] + [shift(halo_own, "mp", k, True) for k in range(1, mp)]
    lower, upper = hidden[:part_rows], hidden[part_rows:]
    low_blocks = [shift(lower, "mp", k, True) for k in range(1, mp)]
    upper, *low_blocks = lax.optimization_barrier((upper, *low_blocks))
    high_blocks = [shift(upper, "mp", k, True) for k in range(1, mp)]
    blocks = ([lower] + low_blocks, [upper] + high_blocks)

    place = jnp.arange(model, dtype=jnp.int32)
    came = lax.rem(me - place // width + mp, mp) * width + lax.rem(place, width)
    columns = jnp.arange(model, dtype=jnp.int32)[None, :]
    pick_f = (came[:, None] == columns).astype(BF16)
    pick_r = (model - 1 - came[:, None] == columns).astype(BF16)
    w_in = jnp.concatenate([w_x, w_bc, w_z], axis=1)
    w_f = jnp.dot(pick_f, w_in, preferred_element_type=F32).astype(BF16)
    w_r = jnp.dot(pick_r, w_in, preferred_element_type=F32).astype(BF16)
    pad = 8 - heads
    dt_pad = jnp.pad(w_dt, ((0, 0), (0, pad)))
    dt_t = lax.dot_general(
        dt_pad,
        jnp.concatenate([pick_f, pick_r], axis=0),
        (((0,), (1,)), ((), ())),
        preferred_element_type=F32,
    ).astype(BF16)
    w_dt2 = jnp.concatenate([dt_t[:, :model], dt_t[:, model:]], axis=0)
    goes = lax.rem(me + place // width, mp) * width + lax.rem(place, width)
    out_f = jnp.dot(
        w_out, (columns.T == goes[None, :]).astype(BF16), preferred_element_type=F32
    ).astype(BF16)
    out_r = jnp.dot(
        w_out, (columns.T == model - 1 - goes[None, :]).astype(BF16), preferred_element_type=F32
    ).astype(BF16)

    bounds = jnp.cumsum(piece_lengths).astype(jnp.int32)
    first_row = (lax.axis_index("ctx") * rows).astype(jnp.int32)[None]
    sms = [jnp.concatenate([bounds, first_row + half * part_rows]) for half in (0, 1)]
    conv_w = jnp.pad(jnp.concatenate([conv_x, conv_bc], axis=1), ((0, 4), (0, 0)))
    bias = jnp.pad(dt_bias, (0, pad))
    rate = jnp.pad(-LOG2E * decay_rate, (0, pad))
    head_par = jnp.broadcast_to(
        jnp.concatenate([bias, bias, rate, rate])[:, None], (32, SUB)
    ).astype(F32)
    owner = jnp.arange(inner, dtype=jnp.int32)[None, :] // HEAD_DIM
    e1 = (jnp.arange(8, dtype=jnp.int32)[:, None] == owner).astype(F32)
    e2 = jnp.concatenate([e1, e1], axis=0).astype(BF16)
    skip8 = jnp.broadcast_to(jnp.repeat(skip_gain, HEAD_DIM)[None, :], (8, inner))
    gain8 = jnp.broadcast_to(norm_gain[None, :], (8, inner))

    smem = pl.BlockSpec(memory_space=pltpu.SMEM)

    def whole(shape):
        return pl.BlockSpec(shape, lambda i: (0,) * len(shape))

    def up(cols):
        return pl.BlockSpec((CHUNK, cols), lambda i: (i, 0))

    def down(cols):
        return pl.BlockSpec((CHUNK, cols), lambda i: (nc - 1 - i, 0))

    aux_up = pl.BlockSpec((1, 64, SUB), lambda i: (i, 0, 0))
    aux_down = pl.BlockSpec((1, 64, SUB), lambda i: (nc - 1 - i, 0, 0))
    st_up = pl.BlockSpec((2, NSTATE, inner), lambda i: (i, 0, 0))
    st_down = pl.BlockSpec((2, NSTATE, inner), lambda i: (nc - 1 - i, 0, 0))

    def sds(shape, dtype):
        return jax.ShapeDtypeStruct(shape, dtype)

    stream_shapes = [
        sds((part_rows, inner), BF16),
        sds((part_rows, 2 * NSTATE), BF16),
        sds((part_rows, inner), BF16),
        sds((nc, 64, SUB), F32),
        sds((2 * nc, NSTATE, inner), BF16),
    ]
    project = pl.pallas_call(
        functools.partial(project_kernel, nc, mp, inner, pieces),
        grid=(nc,),
        in_specs=[smem]
        + [up(width)] * mp
        + [down(width)] * mp
        + [whole((32, width))] * mp
        + [
            whole((model, mixing + inner)),
            whole((model, mixing + inner)),
            whole((16, model)),
            whole((8, mixing)),
            whole((32, SUB)),
            whole((8, inner)),
            whole((16, inner)),
        ],
        out_specs=[up(inner), up(2 * NSTATE), up(inner), aux_up, st_up]
        + [down(inner), down(2 * NSTATE), down(inner), aux_down, st_down]
        + [whole((NSTATE, inner))] * 2
        + [whole((8, inner))] * 2,
        out_shape=stream_shapes
        + stream_shapes
        + [sds((NSTATE, inner), F32)] * 2
        + [sds((8, inner), F32)] * 2,
        scratch_shapes=[
            pltpu.VMEM((CHUNK + 8, mixing), F32),
            pltpu.VMEM((CHUNK + 8, mixing), F32),
            pltpu.VMEM((NSTATE, inner), F32),
            pltpu.VMEM((NSTATE, inner), F32),
            pltpu.VMEM((8, inner), F32),
            pltpu.VMEM((8, inner), F32),
        ],
        compiler_params=params,
        cost_estimate=cost(4 * part_rows * model * (mixing + inner), 10 << 20),
        name="project",
    )
    made = [
        project(
            sms[half], *blocks[half], *blocks[half],
            *[h[half * 32 : half * 32 + 32] for h in halos],
            w_f, w_r, w_dt2, conv_w, head_par, e1, e2,
        )
        for half in (0, 1)
    ]

    count = lax.axis_size("ctx")
    rounds = rounds_of(count // 2)
    slots = 2 * sum(len(r) for r in rounds)
    packed = NSTATE // 2 + 16
    vmem = pl.BlockSpec(memory_space=pltpu.VMEM)
    *mixed, into_f, into_r = pl.pallas_call(
        functools.partial(exchange_kernel, count, nc, heads, pieces),
        in_specs=[smem] + [vmem] * 21,
        out_specs=[vmem] * 6,
        out_shape=[sds((part_rows, inner), BF16)] * 4 + [sds((2, NSTATE, inner), F32)] * 2,
        scratch_shapes=[
            pltpu.VMEM((2, NSTATE, inner), F32),
            pltpu.VMEM((2, 8, inner), F32),
            pltpu.VMEM((2, NSTATE // 2, inner), F32),
            pltpu.VMEM((2, 8, inner), F32),
            pltpu.VMEM((2, NSTATE, inner), F32),
            pltpu.VMEM((2, NSTATE + 16, inner), BF16),
            pltpu.VMEM((2, NSTATE + 16, inner), BF16),
            pltpu.VMEM((2 * len(rounds), packed, inner), BF16),
            pltpu.VMEM((slots, packed, inner), BF16),
            pltpu.VMEM((2, NSTATE // 2, inner), BF16),
            pltpu.VMEM((2, NSTATE // 2, inner), BF16),
            pltpu.SemaphoreType.DMA((4,)),
            pltpu.SemaphoreType.DMA((slots,)),
            pltpu.SemaphoreType.DMA((slots,)),
            pltpu.SemaphoreType.DMA((4,)),
        ],
        compiler_params=pltpu.CompilerParams(
            vmem_limit_bytes=VMEM_LIMIT, collective_id=0, has_side_effects=True
        ),
        cost_estimate=cost(40 * rows * SUB * inner, 16 << 20, 2 * rows * SUB * heads),
        name="exchange",
    )(
        sms[0],
        skip8,
        *[
            value
            for m in made
            for value in (*m[10:14], m[0], m[1], m[3], m[5], m[6], m[8])
        ],
    )

    finish = pl.pallas_call(
        functools.partial(finish_kernel, nc, inner),
        grid=(nc,),
        in_specs=[up(inner), up(inner), up(2 * NSTATE), aux_up, st_up, whole((NSTATE, inner))]
        + [down(inner), down(inner), down(2 * NSTATE), aux_down, st_down, whole((NSTATE, inner))]
        + [whole((8, inner)), whole((8, inner)), whole((16, inner))],
        out_specs=[
            up(inner),
            pl.BlockSpec((8, CHUNK), lambda i: (0, i)),
            down(inner),
            pl.BlockSpec((8, CHUNK), lambda i: (0, nc - 1 - i)),
        ],
        out_shape=[sds((part_rows, inner), BF16), sds((8, part_rows), F32)] * 2,
        scratch_shapes=[pltpu.VMEM((1, inner), F32)] * 2,
        compiler_params=params,
        cost_estimate=cost(4 * part_rows * NSTATE * inner, 12 << 20),
        name="finish",
    )
    output = pl.pallas_call(
        functools.partial(output_kernel, mp, inner * mp),
        grid=(nc,),
        in_specs=[
            pl.BlockSpec((8, CHUNK), lambda i: (0, i)),
            up(inner),
            up(inner),
            whole((inner, model)),
            whole((inner, model)),
        ],
        out_specs=[up(width)] * mp,
        out_shape=[sds((part_rows, width), F32)] + [sds((part_rows, width), BF16)] * (mp - 1),
        compiler_params=params,
        cost_estimate=cost(4 * part_rows * inner * model, 4 << 20),
        name="output",
    )
    forward_rows = jnp.arange(8, dtype=jnp.int32)[:, None] < 4
    gated, squares = [], []
    for half, m in enumerate(made):
        gated_f, square_f, gated_r, square_r = finish(
            mixed[2 * half], m[2], m[1], m[3], m[4], into_f[half],
            mixed[2 * half + 1], m[7], m[6], m[8], m[9], into_r[half],
            gain8, e1, e2,
        )
        gated.append((gated_f, gated_r))
        squares.append(jnp.where(forward_rows, square_f, square_r))
    other = [[shift(sq, "mp", k, True) for k in range(1, mp)] for sq in squares]
    totals = [sum(got, sq) for got, sq in zip(other, squares)]
    first = output(totals[0], *gated[0], out_f, out_r)
    first, totals[1] = lax.optimization_barrier((first, totals[1]))
    results = []
    for parts in (first, output(totals[1], *gated[1], out_f, out_r)):
        result = parts[0]
        for k in range(1, mp):
            result = result + shift(parts[k], "mp", k, True).astype(F32)
        results.append(result.astype(BF16))
    return jnp.concatenate(results, axis=0)


def solution(mesh):
    return jax.shard_map(
        shards,
        mesh=mesh,
        in_specs=(
            P("ctx", "mp"), P(None, "mp"), P(None, "mp"), P(), P(None, "mp"), P(None, "mp"), P(),
            P("mp"), P("mp"), P("mp"), P("mp"), P("mp", None), P(),
        ),
        out_specs=P("ctx", "mp"),
        check_vma=False,
    )
```

```python
import functools
import jax
import jax.numpy as jnp
from jax import lax
from jax.experimental import pallas as pl
from jax.experimental.pallas import tpu as pltpu
from jax.sharding import PartitionSpec as P

HEAD_DIM = 64
NSTATE = 128
SUB = 128
CHUNK = 256
EPSILON = 1e-05
LOG2E = 1.4426950408889634
F32 = jnp.float32
BF16 = jnp.bfloat16
BIG = 1 << 30
VMEM_LIMIT = 28 * 1024 * 1024

NT = (((1,), (1,)), ((), ()))
TN = (((0,), (0,)), ((), ()))


def piece_start(sm, pieces, pos):
    out = jnp.zeros_like(pos)
    for k in range(pieces):
        bound = sm[k]
        out = jnp.maximum(out, jnp.where(pos >= bound, bound, 0))
    return out


def piece_end(sm, pieces, pos):
    out = jnp.full_like(pos, BIG)
    for k in range(pieces):
        bound = sm[k]
        out = jnp.minimum(out, jnp.where(pos < bound, bound, BIG))
    return out


def silu(value):
    half = 0.5 * value
    return half * jnp.tanh(half) + half


def expand_rows(weights, expander2):
    high = weights.astype(BF16)
    low = (weights - high.astype(F32)).astype(BF16)
    both = jnp.concatenate([high, low], axis=0)
    return lax.dot_general(both, expander2, TN, preferred_element_type=F32)


def project_kernel(nc, mp, inner, pieces, *refs):
    sm = refs[0]
    hf, hr, halo = refs[1 : 1 + mp], refs[1 + mp : 1 + 2 * mp], refs[1 + 2 * mp : 1 + 3 * mp]
    (wf, wr, wdt, cw, head_par, e1, e2) = refs[1 + 3 * mp : 8 + 3 * mp]
    outs = refs[8 + 3 * mp : 22 + 3 * mp]
    buf_f, buf_r, st_f, st_r, dec_f, dec_r = refs[22 + 3 * mp :]
    step = pl.program_id(0)
    base = sm[pieces]
    mixing = inner + 2 * NSTATE
    width = wf.shape[0] // mp

    def dots(blocks, weight, columns):
        total = None
        for b in range(mp):
            part = jnp.dot(
                blocks[b], weight[b * width : (b + 1) * width, columns], preferred_element_type=F32
            )
            total = part if total is None else total + part
        return total

    @pl.when(step == 0)
    def _():
        low = dots([h[0:16, :] for h in halo], wf, slice(0, mixing))
        high = dots([h[16:32, :] for h in halo], wr, slice(0, mixing))
        buf_f[0:8, :] = low[8:16].astype(BF16).astype(F32)
        buf_r[CHUNK : CHUNK + 8, :] = high[0:8].astype(BF16).astype(F32)
        st_f[...] = jnp.zeros_like(st_f)
        st_r[...] = jnp.zeros_like(st_r)
        dec_f[...] = jnp.ones_like(dec_f)
        dec_r[...] = jnp.ones_like(dec_r)

    @pl.when(step > 0)
    def _():
        buf_f[0:8, :] = buf_f[CHUNK : CHUNK + 8, :]
        buf_r[CHUNK : CHUNK + 8, :] = buf_r[0:8, :]

    rows = lax.broadcasted_iota(jnp.int32, (SUB, SUB), 0)
    lanes = lax.broadcasted_iota(jnp.int32, (SUB, SUB), 1)
    for forward in (True, False):
        blocks = [h[...] for h in (hf if forward else hr)]
        weight = wf if forward else wr
        buf = buf_f if forward else buf_r
        state, decay = (st_f, dec_f) if forward else (st_r, dec_r)
        x_out, bc_out, z_out, aux_out, before_out = outs[:5] if forward else outs[5:10]
        chunk = step if forward else nc - 1 - step
        first = base + chunk * CHUNK
        own = 8 if forward else 0
        buf[own : own + CHUNK, :] = (
            dots(blocks, weight, slice(0, mixing)).astype(BF16).astype(F32)
        )
        z_out[...] = dots(blocks, weight, slice(mixing, mixing + inner)).astype(BF16)

        raw = None
        lo = 0 if forward else 8
        for b in range(mp):
            part = lax.dot_general(
                wdt[lo : lo + 8, b * width : (b + 1) * width],
                blocks[b],
                NT,
                preferred_element_type=F32,
            )
            raw = part if raw is None else raw + part
        raw = raw.astype(BF16).astype(F32)
        raw = jnp.concatenate([raw[:, :SUB], raw[:, SUB:]], axis=0)
        par = head_par[...]
        shifted = raw + par[0:16]
        step_dt = jnp.maximum(shifted, 0.0) + jnp.log1p(jnp.exp(-jnp.abs(shifted)))
        log_decay = step_dt * par[16:32]
        tri = jnp.where(rows <= lanes if forward else rows >= lanes, 1.0, 0.0).astype(F32)
        cum = jnp.dot(
            log_decay, tri, precision=lax.Precision.HIGHEST, preferred_element_type=F32
        )
        total = cum[:, SUB - 1 : SUB] if forward else cum[:, 0:1]
        block_first = first + SUB * (lax.broadcasted_iota(jnp.int32, (16, SUB), 0) // 8)
        position = block_first + lax.broadcasted_iota(jnp.int32, (16, SUB), 1)
        start = piece_start(sm, pieces, position)
        end = piece_end(sm, pieces, position)
        block_last = block_first + SUB - 1
        if forward:
            to_end_ok = end > block_last
            from_start_ok = start < block_first
            whole_ok = piece_start(sm, pieces, block_last) < block_first
        else:
            to_end_ok = start <= block_first
            from_start_ok = end > block_last + 1
            whole_ok = piece_end(sm, pieces, block_first) > block_last + 1
        to_end = jnp.where(to_end_ok, jnp.exp2(total - cum) * step_dt, 0.0)
        from_start = jnp.where(from_start_ok, jnp.exp2(cum), 0.0)
        whole = jnp.where(whole_ok, jnp.exp2(jnp.broadcast_to(total, cum.shape)), 0.0)
        aux_out[0, 0:16, :] = cum
        aux_out[0, 16:32, :] = cum - jnp.log2(step_dt)
        aux_out[0, 32:48, :] = from_start
        aux_out[0, 48:64, :] = whole

        for b in (0, 1) if forward else (1, 0):
            at = first + b * SUB + rows
            if forward:
                room = at - piece_start(sm, pieces, at)
            else:
                room = piece_end(sm, pieces, at) - 1 - at
            same = [None] + [room >= j for j in (1, 2, 3)]
            r0 = own + b * SUB
            out_rows = slice(b * SUB, (b + 1) * SUB)
            for g in range(mixing // 128):
                cols = slice(g * 128, (g + 1) * 128)
                acc = buf[r0 : r0 + SUB, cols] * cw[3:4, cols]
                for j in (1, 2, 3):
                    off = r0 - j if forward else r0 + j
                    tap = buf[off : off + SUB, cols] * cw[3 - j : 4 - j, cols]
                    acc = acc + jnp.where(same[j], tap, 0.0)
                value = silu(acc).astype(BF16)
                if g * 128 < inner:
                    x_out[out_rows, cols] = value
                else:
                    bc_out[out_rows, slice(g * 128 - inner, g * 128 - inner + 128)] = value
            hb = slice(b * 8, b * 8 + 8)
            weights = expand_rows(to_end[hb], e2[...])
            scaled = (x_out[out_rows, :].astype(F32) * weights).astype(BF16)
            added = lax.dot_general(
                bc_out[out_rows, 0:NSTATE], scaled, TN, preferred_element_type=F32
            )
            grow = jnp.sum(whole[hb, 0:1] * e1[...], axis=0, keepdims=True)
            held = state[...]
            before_out[b] = held.astype(BF16)
            state[...] = held * grow + added
            decay[...] = decay[...] * grow

    outs[10][...] = st_f[...]
    outs[11][...] = st_r[...]
    outs[12][...] = dec_f[...]
    outs[13][...] = dec_r[...]


def intra_rows(forward, heads, pieces, sm, x_ref, bc_ref, aux_ref, skip_ref, y_ref, offset, chunk):
    base = sm[pieces] + offset
    rows = lax.broadcasted_iota(jnp.int32, (SUB, SUB), 0)
    lanes = lax.broadcasted_iota(jnp.int32, (SUB, SUB), 1)
    left = lanes < HEAD_DIM
    aux = aux_ref[chunk]
    for b in (0, 1):
        at = pl.ds(pl.multiple_of(chunk * CHUNK + b * SUB, SUB), SUB)
        begin = base + chunk * CHUNK + b * SUB
        if forward:
            mask = (lanes <= rows) & (begin + lanes >= piece_start(sm, pieces, begin + rows))
        else:
            mask = (lanes >= rows) & (begin + lanes < piece_end(sm, pieces, begin + rows))
        scores = lax.dot_general(
            bc_ref[at, NSTATE:], bc_ref[at, 0:NSTATE], NT, preferred_element_type=F32
        )
        cum_t = aux[b * 8 : b * 8 + 8, :].T
        cum_s = aux[16 + b * 8 : 16 + b * 8 + 8, :]
        for pair in range(heads // 2):
            cols = slice(pair * 128, (pair + 1) * 128)
            xf = x_ref[at, cols].astype(F32)
            parts = []
            for h in (2 * pair, 2 * pair + 1):
                gap = jnp.where(mask, cum_t[:, h : h + 1] - cum_s[h : h + 1, :], -1e30)
                parts.append((jnp.exp2(gap) * scores).astype(BF16))
            stacked = jnp.concatenate(
                [
                    jnp.where(left, xf, 0.0).astype(BF16),
                    jnp.where(left, 0.0, xf).astype(BF16),
                ],
                axis=0,
            )
            mixed = jnp.dot(
                jnp.concatenate(parts, axis=1), stacked, preferred_element_type=F32
            )
            y_ref[at, cols] = (mixed + skip_ref[0:1, cols] * xf).astype(BF16)


def rounds_of(count):
    rounds, window = [], 1
    while 4 * window < count - 1:
        rounds.append([window * k for k in (1, 2, 3)])
        window *= 4
    rounds.append([1 + window * k for k in range(-(-(count - 1) // window))])
    return rounds


def exchange_kernel(count, nc, heads, pieces, *refs):
    sm, skip = refs[:2]
    halves = (refs[2:12], refs[12:22])
    mixed = (refs[22:24], refs[24:26])
    into_f, into_r = refs[26:28]
    own, own_fade, held, fade, full = refs[28:33]
    pair_sent, pair_landed, sent, landed, last_sent, last_landed = refs[33:39]
    pair_sems, send_sem, recv_sem, last_sems = refs[39:]
    (st_f0, st_r0, dec_f0, dec_r0), (st_f1, st_r1, dec_f1, dec_r1) = (h[:4] for h in halves)
    index = lax.axis_index("ctx")
    core = lax.rem(index, 2)
    sibling = {"ctx": index + 1 - 2 * core}
    rounds = rounds_of(count // 2)
    signs = (1, -1)
    part = NSTATE // 2
    mine = pl.ds(pl.multiple_of(core * part, part), part)
    theirs = pl.ds(pl.multiple_of((1 - core) * part, part), part)

    def reaches(step):
        return index + step < count if step > 0 else index + step >= 0

    def send(src, dst, send_at, recv_at, target):
        return pltpu.make_async_remote_copy(
            src_ref=src,
            dst_ref=dst,
            send_sem=send_at,
            recv_sem=recv_at,
            device_id=target,
            device_id_type=pl.DeviceIdType.MESH,
        )

    def signal(target):
        pl.semaphore_signal(barrier, inc=1, device_id=target, device_id_type=pl.DeviceIdType.MESH)

    def pack_decay(decay):
        high = decay.astype(BF16)
        return jnp.concatenate([high, (decay - high.astype(F32)).astype(BF16)], axis=0)

    def on_first(shape, yes, no):
        return jnp.where(jnp.full(shape, core, jnp.int32) == 0, yes, no)

    work = [(stream, half) for stream in (0, 1) for half in (0, 1)]

    def compute(pieces_now):
        for stream, half in pieces_now:
            x_ref, bc_ref, aux_ref = halves[half][4 + 3 * stream : 7 + 3 * stream]
            y_ref = mixed[half][stream]

            def body(chunk, carry):
                intra_rows(
                    stream == 0, heads, pieces, sm, x_ref, bc_ref, aux_ref, skip, y_ref,
                    half * nc * CHUNK, chunk,
                )
                return carry

            lax.fori_loop(0, nc, body, 0)

    barrier = pltpu.get_barrier_semaphore()
    steps = sorted({2 * sign * s for r in rounds for s in r for sign in signs})
    signal(sibling)
    for step in steps:

        @pl.when(reaches(step))
        def _(step=step):
            signal({"ctx": index + step})

    peers = 1 + sum(
        1 - lax.div(index + step, count) if step > 0 else lax.div(index + step + count, count)
        for step in steps
    )
    pl.semaphore_wait(barrier, peers)

    own[0] = st_f0[...] * dec_f1[0:1, :] + st_f1[...]
    own[1] = st_r1[...] * dec_r0[0:1, :] + st_r0[...]
    own_fade[0] = dec_f0[...] * dec_f1[...]
    own_fade[1] = dec_r0[...] * dec_r1[...]
    swaps = []
    for stream in (0, 1):
        pair_sent[stream, 0:NSTATE, :] = own[stream].astype(BF16)
        pair_sent[stream, NSTATE : NSTATE + 16, :] = pack_decay(own_fade[stream])
        swap = send(
            pair_sent.at[stream], pair_landed.at[stream],
            pair_sems.at[stream], pair_sems.at[2 + stream], sibling,
        )
        swap.start()
        swaps.append(swap)
    compute(work[0:1])
    for swap in swaps:
        swap.wait()
    shape = held.shape[1:]
    for stream in (0, 1):
        tail = pair_landed[stream, NSTATE : NSTATE + 16, :].astype(F32)
        other_fade = tail[0:8] + tail[8:16]
        other = pair_landed[stream, mine, :].astype(F32)
        here = own[stream, mine, :]
        before = other_fade[0:1] * here + other
        after = own_fade[stream, 0:1, :] * other + here
        held[stream] = on_first(shape, *((before, after) if stream == 0 else (after, before)))
        fade[stream] = own_fade[stream] * other_fade

    slot = 0
    for number, shifts in enumerate(rounds):
        last = number == len(rounds) - 1
        copies = []
        for stream, sign in enumerate(signs):
            at = number * 2 + stream
            sent[at, 0:part, :] = held[stream].astype(BF16)
            sent[at, part : part + 16, :] = pack_decay(fade[stream])
            for s in shifts:
                step = 2 * sign * s
                copy = send(
                    sent.at[at], landed.at[slot],
                    send_sem.at[slot], recv_sem.at[slot], {"ctx": index + step},
                )
                copies.append((stream, step, slot, copy))
                slot += 1

                @pl.when(reaches(step))
                def _(copy=copy):
                    copy.start()

        if len(rounds) == 1:
            compute(work[1:])
        elif number == 0:
            compute(work[1:3])
        elif number == 1:
            compute(work[3:])
        if last:
            held[...] = jnp.zeros_like(held)
            fade[...] = jnp.ones_like(fade)
        for stream, step, at, copy in copies:

            @pl.when(reaches(-step))
            def _(stream=stream, at=at, copy=copy):
                copy.wait_recv()
                more = landed[at, 0:part, :].astype(F32)
                tail = landed[at, part : part + 16, :].astype(F32)
                held[stream] = held[stream] + fade[stream, 0:1, :] * more
                fade[stream] = fade[stream] * (tail[0:8] + tail[8:16])

        for stream, step, at, copy in copies:

            @pl.when(reaches(step))
            def _(copy=copy):
                copy.wait_send()

    swaps = []
    for stream in (0, 1):
        last_sent[stream] = held[stream].astype(BF16)
        swap = send(
            last_sent.at[stream], last_landed.at[stream],
            last_sems.at[stream], last_sems.at[2 + stream], sibling,
        )
        swap.start()
        swaps.append(swap)
    for stream in (0, 1):
        swaps[stream].wait()
        full[stream, mine, :] = held[stream]
        full[stream, theirs, :] = last_landed[stream].astype(F32)
        tail = pair_landed[stream, NSTATE : NSTATE + 16, :].astype(F32)
        outer = full[stream]
        passed = (tail[0:1] + tail[8:9]) * outer + pair_landed[stream, 0:NSTATE, :].astype(F32)
        into = on_first(
            outer.shape, *((outer, passed) if stream == 0 else (passed, outer))
        )
        if stream == 0:
            into_f[0] = into
            into_f[1] = st_f0[...] + dec_f0[0:1, :] * into
        else:
            into_r[0] = st_r1[...] + dec_r1[0:1, :] * into
            into_r[1] = into


def finish_kernel(nc, inner, *refs):
    ins, par = refs[0:12], refs[12:15]
    outs = refs[15:19]
    grown = refs[19:21]
    gain_ref, e1, e2 = par
    step = pl.program_id(0)

    @pl.when(step == 0)
    def _():
        grown[0][...] = jnp.ones_like(grown[0])
        grown[1][...] = jnp.ones_like(grown[1])

    ones = jnp.ones((8, inner), BF16)
    for stream in (0, 1):
        y_ref, z_ref, bc_ref, aux_ref, before_ref, into_ref = ins[stream * 6 : stream * 6 + 6]
        g_out, ss_out = outs[stream * 2 : stream * 2 + 2]
        into = into_ref[...]
        for b in (0, 1) if stream == 0 else (1, 0):
            at = slice(b * SUB, (b + 1) * SUB)
            grow = grown[stream][...]
            state = (before_ref[b].astype(F32) + grow * into).astype(BF16)
            factor = expand_rows(aux_ref[0, 32 + b * 8 : 40 + b * 8, :], e2[...])
            inter = jnp.dot(bc_ref[at, NSTATE:], state, preferred_element_type=F32)
            mixed = y_ref[at, :].astype(F32) + inter * factor
            gated = mixed * silu(z_ref[at, :].astype(F32))
            ss_out[:, at] = lax.dot_general(
                ones, (gated * gated).astype(BF16), NT, preferred_element_type=F32
            )
            g_out[at, :] = (gated * gain_ref[0:1, :]).astype(BF16)
            whole = aux_ref[0, 48 + b * 8 : 56 + b * 8, 0:1]
            grown[stream][...] = grow * jnp.sum(whole * e1[...], axis=0, keepdims=True)


def output_kernel(mp, total_width, ss_ref, gf_ref, gr_ref, wf_ref, wr_ref, *outs):
    factor = lax.rsqrt(ss_ref[...] * (1.0 / total_width) + EPSILON).T
    width = wf_ref.shape[1] // mp
    for k in range(mp):
        cols = slice(k * width, (k + 1) * width)
        part = factor[:, 0:1] * jnp.dot(gf_ref[...], wf_ref[:, cols], preferred_element_type=F32)
        part = part + factor[:, 4:5] * jnp.dot(
            gr_ref[...], wr_ref[:, cols], preferred_element_type=F32
        )
        outs[k][...] = part.astype(outs[k].dtype)


def shift(value, axis, by, wrap):
    count = lax.axis_size(axis)
    if wrap:
        pairs = [(i, (i + by) % count) for i in range(count)]
    else:
        pairs = [(i, i + by) for i in range(count) if 0 <= i + by < count]
    return lax.ppermute(value, axis, pairs)


def cost(flops, size, trans=0):
    return pl.CostEstimate(flops=flops, bytes_accessed=size, transcendentals=trans)


def shards(
    hidden, w_x, w_z, w_bc, w_dt, conv_x, conv_bc, dt_bias, decay_rate, skip_gain, norm_gain,
    w_out, piece_lengths,
):
    mp = lax.axis_size("mp")
    me = lax.axis_index("mp")
    rows, width = hidden.shape
    model = width * mp
    heads = dt_bias.shape[0]
    inner = heads * HEAD_DIM
    mixing = inner + 2 * NSTATE
    pieces = piece_lengths.shape[0]
    part_rows = rows // 2
    nc = part_rows // CHUNK
    params = pltpu.CompilerParams(vmem_limit_bytes=VMEM_LIMIT)

    from_below = shift(hidden[rows - 16 :], "ctx", 1, False)
    from_above = shift(hidden[:16], "ctx", -1, False)
    halo_own = jnp.concatenate(
        [
            from_below,
            hidden[part_rows : part_rows + 16],
            hidden[part_rows - 16 : part_rows],
            from_above,
        ],
        axis=0,
    )
    halos = [halo_own] + [shift(halo_own, "mp", k, True) for k in range(1, mp)]
    lower, upper = hidden[:part_rows], hidden[part_rows:]
    low_blocks = [shift(lower, "mp", k, True) for k in range(1, mp)]
    upper, *low_blocks = lax.optimization_barrier((upper, *low_blocks))
    high_blocks = [shift(upper, "mp", k, True) for k in range(1, mp)]
    blocks = ([lower] + low_blocks, [upper] + high_blocks)

    place = jnp.arange(model, dtype=jnp.int32)
    came = lax.rem(me - place // width + mp, mp) * width + lax.rem(place, width)
    columns = jnp.arange(model, dtype=jnp.int32)[None, :]
    pick_f = (came[:, None] == columns).astype(BF16)
    pick_r = (model - 1 - came[:, None] == columns).astype(BF16)
    w_in = jnp.concatenate([w_x, w_bc, w_z], axis=1)
    w_f = jnp.dot(pick_f, w_in, preferred_element_type=F32).astype(BF16)
    w_r = jnp.dot(pick_r, w_in, preferred_element_type=F32).astype(BF16)
    pad = 8 - heads
    dt_pad = jnp.pad(w_dt, ((0, 0), (0, pad)))
    dt_t = lax.dot_general(
        dt_pad,
        jnp.concatenate([pick_f, pick_r], axis=0),
        (((0,), (1,)), ((), ())),
        preferred_element_type=F32,
    ).astype(BF16)
    w_dt2 = jnp.concatenate([dt_t[:, :model], dt_t[:, model:]], axis=0)
    goes = lax.rem(me + place // width, mp) * width + lax.rem(place, width)
    out_f = jnp.dot(
        w_out, (columns.T == goes[None, :]).astype(BF16), preferred_element_type=F32
    ).astype(BF16)
    out_r = jnp.dot(
        w_out, (columns.T == model - 1 - goes[None, :]).astype(BF16), preferred_element_type=F32
    ).astype(BF16)

    bounds = jnp.cumsum(piece_lengths).astype(jnp.int32)
    first_row = (lax.axis_index("ctx") * rows).astype(jnp.int32)[None]
    sms = [jnp.concatenate([bounds, first_row + half * part_rows]) for half in (0, 1)]
    conv_w = jnp.pad(jnp.concatenate([conv_x, conv_bc], axis=1), ((0, 4), (0, 0)))
    bias = jnp.pad(dt_bias, (0, pad))
    rate = jnp.pad(-LOG2E * decay_rate, (0, pad))
    head_par = jnp.broadcast_to(
        jnp.concatenate([bias, bias, rate, rate])[:, None], (32, SUB)
    ).astype(F32)
    owner = jnp.arange(inner, dtype=jnp.int32)[None, :] // HEAD_DIM
    e1 = (jnp.arange(8, dtype=jnp.int32)[:, None] == owner).astype(F32)
    e2 = jnp.concatenate([e1, e1], axis=0).astype(BF16)
    skip8 = jnp.broadcast_to(jnp.repeat(skip_gain, HEAD_DIM)[None, :], (8, inner))
    gain8 = jnp.broadcast_to(norm_gain[None, :], (8, inner))

    smem = pl.BlockSpec(memory_space=pltpu.SMEM)

    def whole(shape):
        return pl.BlockSpec(shape, lambda i: (0,) * len(shape))

    def up(cols):
        return pl.BlockSpec((CHUNK, cols), lambda i: (i, 0))

    def down(cols):
        return pl.BlockSpec((CHUNK, cols), lambda i: (nc - 1 - i, 0))

    aux_up = pl.BlockSpec((1, 64, SUB), lambda i: (i, 0, 0))
    aux_down = pl.BlockSpec((1, 64, SUB), lambda i: (nc - 1 - i, 0, 0))
    st_up = pl.BlockSpec((2, NSTATE, inner), lambda i: (i, 0, 0))
    st_down = pl.BlockSpec((2, NSTATE, inner), lambda i: (nc - 1 - i, 0, 0))

    def sds(shape, dtype):
        return jax.ShapeDtypeStruct(shape, dtype)

    stream_shapes = [
        sds((part_rows, inner), BF16),
        sds((part_rows, 2 * NSTATE), BF16),
        sds((part_rows, inner), BF16),
        sds((nc, 64, SUB), F32),
        sds((2 * nc, NSTATE, inner), BF16),
    ]
    project = pl.pallas_call(
        functools.partial(project_kernel, nc, mp, inner, pieces),
        grid=(nc,),
        in_specs=[smem]
        + [up(width)] * mp
        + [down(width)] * mp
        + [whole((32, width))] * mp
        + [
            whole((model, mixing + inner)),
            whole((model, mixing + inner)),
            whole((16, model)),
            whole((8, mixing)),
            whole((32, SUB)),
            whole((8, inner)),
            whole((16, inner)),
        ],
        out_specs=[up(inner), up(2 * NSTATE), up(inner), aux_up, st_up]
        + [down(inner), down(2 * NSTATE), down(inner), aux_down, st_down]
        + [whole((NSTATE, inner))] * 2
        + [whole((8, inner))] * 2,
        out_shape=stream_shapes
        + stream_shapes
        + [sds((NSTATE, inner), F32)] * 2
        + [sds((8, inner), F32)] * 2,
        scratch_shapes=[
            pltpu.VMEM((CHUNK + 8, mixing), F32),
            pltpu.VMEM((CHUNK + 8, mixing), F32),
            pltpu.VMEM((NSTATE, inner), F32),
            pltpu.VMEM((NSTATE, inner), F32),
            pltpu.VMEM((8, inner), F32),
            pltpu.VMEM((8, inner), F32),
        ],
        compiler_params=params,
        cost_estimate=cost(4 * part_rows * model * (mixing + inner), 10 << 20),
        name="project",
    )
    made = [
        project(
            sms[half], *blocks[half], *blocks[half],
            *[h[half * 32 : half * 32 + 32] for h in halos],
            w_f, w_r, w_dt2, conv_w, head_par, e1, e2,
        )
        for half in (0, 1)
    ]

    count = lax.axis_size("ctx")
    rounds = rounds_of(count // 2)
    slots = 2 * sum(len(r) for r in rounds)
    packed = NSTATE // 2 + 16
    vmem = pl.BlockSpec(memory_space=pltpu.VMEM)
    *mixed, into_f, into_r = pl.pallas_call(
        functools.partial(exchange_kernel, count, nc, heads, pieces),
        in_specs=[smem] + [vmem] * 21,
        out_specs=[vmem] * 6,
        out_shape=[sds((part_rows, inner), BF16)] * 4 + [sds((2, NSTATE, inner), F32)] * 2,
        scratch_shapes=[
            pltpu.VMEM((2, NSTATE, inner), F32),
            pltpu.VMEM((2, 8, inner), F32),
            pltpu.VMEM((2, NSTATE // 2, inner), F32),
            pltpu.VMEM((2, 8, inner), F32),
            pltpu.VMEM((2, NSTATE, inner), F32),
            pltpu.VMEM((2, NSTATE + 16, inner), BF16),
            pltpu.VMEM((2, NSTATE + 16, inner), BF16),
            pltpu.VMEM((2 * len(rounds), packed, inner), BF16),
            pltpu.VMEM((slots, packed, inner), BF16),
            pltpu.VMEM((2, NSTATE // 2, inner), BF16),
            pltpu.VMEM((2, NSTATE // 2, inner), BF16),
            pltpu.SemaphoreType.DMA((4,)),
            pltpu.SemaphoreType.DMA((slots,)),
            pltpu.SemaphoreType.DMA((slots,)),
            pltpu.SemaphoreType.DMA((4,)),
        ],
        compiler_params=pltpu.CompilerParams(
            vmem_limit_bytes=VMEM_LIMIT, collective_id=0, has_side_effects=True
        ),
        cost_estimate=cost(40 * rows * SUB * inner, 16 << 20, 2 * rows * SUB * heads),
        name="exchange",
    )(
        sms[0],
        skip8,
        *[
            value
            for m in made
            for value in (*m[10:14], m[0], m[1], m[3], m[5], m[6], m[8])
        ],
    )

    finish = pl.pallas_call(
        functools.partial(finish_kernel, nc, inner),
        grid=(nc,),
        in_specs=[up(inner), up(inner), up(2 * NSTATE), aux_up, st_up, whole((NSTATE, inner))]
        + [down(inner), down(inner), down(2 * NSTATE), aux_down, st_down, whole((NSTATE, inner))]
        + [whole((8, inner)), whole((8, inner)), whole((16, inner))],
        out_specs=[
            up(inner),
            pl.BlockSpec((8, CHUNK), lambda i: (0, i)),
            down(inner),
            pl.BlockSpec((8, CHUNK), lambda i: (0, nc - 1 - i)),
        ],
        out_shape=[sds((part_rows, inner), BF16), sds((8, part_rows), F32)] * 2,
        scratch_shapes=[pltpu.VMEM((1, inner), F32)] * 2,
        compiler_params=params,
        cost_estimate=cost(4 * part_rows * NSTATE * inner, 12 << 20),
        name="finish",
    )
    output = pl.pallas_call(
        functools.partial(output_kernel, mp, inner * mp),
        grid=(nc,),
        in_specs=[
            pl.BlockSpec((8, CHUNK), lambda i: (0, i)),
            up(inner),
            up(inner),
            whole((inner, model)),
            whole((inner, model)),
        ],
        out_specs=[up(width)] * mp,
        out_shape=[sds((part_rows, width), F32)] + [sds((part_rows, width), BF16)] * (mp - 1),
        compiler_params=params,
        cost_estimate=cost(4 * part_rows * inner * model, 4 << 20),
        name="output",
    )
    forward_rows = jnp.arange(8, dtype=jnp.int32)[:, None] < 4
    results = []
    mixed_now = mixed[0:2]
    for half, m in enumerate(made):
        gated_f, square_f, gated_r, square_r = finish(
            mixed_now[0], m[2], m[1], m[3], m[4], into_f[half],
            mixed_now[1], m[7], m[6], m[8], m[9], into_r[half],
            gain8, e1, e2,
        )
        squares = jnp.where(forward_rows, square_f, square_r)
        total = squares
        for k in range(1, mp):
            total = total + shift(squares, "mp", k, True)
        parts = output(total, gated_f, gated_r, out_f, out_r)
        if half == 0:
            parts, mixed_now = lax.optimization_barrier((parts, mixed[2:4]))
        result = parts[0]
        for k in range(1, mp):
            result = result + shift(parts[k], "mp", k, True).astype(F32)
        results.append(result.astype(BF16))
    return jnp.concatenate(results, axis=0)


def solution(mesh):
    return jax.shard_map(
        shards,
        mesh=mesh,
        in_specs=(
            P("ctx", "mp"), P(None, "mp"), P(None, "mp"), P(), P(None, "mp"), P(None, "mp"), P(),
            P("mp"), P("mp"), P("mp"), P("mp"), P("mp", None), P(),
        ),
        out_specs=P("ctx", "mp"),
        check_vma=False,
    )
```

```python
import functools
import jax
import jax.numpy as jnp
from jax import lax
from jax.experimental import pallas as pl
from jax.experimental.pallas import tpu as pltpu
from jax.sharding import PartitionSpec as P

HEAD_DIM = 64
NSTATE = 128
SUB = 128
CHUNK = 256
EPSILON = 1e-05
LOG2E = 1.4426950408889634
F32 = jnp.float32
BF16 = jnp.bfloat16
BIG = 1 << 30
VMEM_LIMIT = 28 * 1024 * 1024

NT = (((1,), (1,)), ((), ()))
TN = (((0,), (0,)), ((), ()))


def piece_start(sm, pieces, pos):
    out = jnp.zeros_like(pos)
    for k in range(pieces):
        bound = sm[k]
        out = jnp.maximum(out, jnp.where(pos >= bound, bound, 0))
    return out


def piece_end(sm, pieces, pos):
    out = jnp.full_like(pos, BIG)
    for k in range(pieces):
        bound = sm[k]
        out = jnp.minimum(out, jnp.where(pos < bound, bound, BIG))
    return out


def silu(value):
    half = 0.5 * value
    return half * jnp.tanh(half) + half


def expand_rows(weights, expander2):
    high = weights.astype(BF16)
    low = (weights - high.astype(F32)).astype(BF16)
    both = jnp.concatenate([high, low], axis=0)
    return lax.dot_general(both, expander2, TN, preferred_element_type=F32)


def project_kernel(nc, mp, inner, pieces, *refs):
    sm = refs[0]
    hf, hr, halo = refs[1 : 1 + mp], refs[1 + mp : 1 + 2 * mp], refs[1 + 2 * mp : 1 + 3 * mp]
    (wf, wr, wdt, cw, head_par, e1, e2) = refs[1 + 3 * mp : 8 + 3 * mp]
    outs = refs[8 + 3 * mp : 22 + 3 * mp]
    buf_f, buf_r, st_f, st_r, dec_f, dec_r = refs[22 + 3 * mp :]
    step = pl.program_id(0)
    base = sm[pieces]
    mixing = inner + 2 * NSTATE
    width = wf.shape[0] // mp

    def dots(blocks, weight, columns):
        total = None
        for b in range(mp):
            part = jnp.dot(
                blocks[b], weight[b * width : (b + 1) * width, columns], preferred_element_type=F32
            )
            total = part if total is None else total + part
        return total

    @pl.when(step == 0)
    def _():
        low = dots([h[0:16, :] for h in halo], wf, slice(0, mixing))
        high = dots([h[16:32, :] for h in halo], wr, slice(0, mixing))
        buf_f[0:8, :] = low[8:16].astype(BF16).astype(F32)
        buf_r[CHUNK : CHUNK + 8, :] = high[0:8].astype(BF16).astype(F32)
        st_f[...] = jnp.zeros_like(st_f)
        st_r[...] = jnp.zeros_like(st_r)
        dec_f[...] = jnp.ones_like(dec_f)
        dec_r[...] = jnp.ones_like(dec_r)

    @pl.when(step > 0)
    def _():
        buf_f[0:8, :] = buf_f[CHUNK : CHUNK + 8, :]
        buf_r[CHUNK : CHUNK + 8, :] = buf_r[0:8, :]

    rows = lax.broadcasted_iota(jnp.int32, (SUB, SUB), 0)
    lanes = lax.broadcasted_iota(jnp.int32, (SUB, SUB), 1)
    for forward in (True, False):
        blocks = [h[...] for h in (hf if forward else hr)]
        weight = wf if forward else wr
        buf = buf_f if forward else buf_r
        state, decay = (st_f, dec_f) if forward else (st_r, dec_r)
        x_out, bc_out, z_out, aux_out, before_out = outs[:5] if forward else outs[5:10]
        chunk = step if forward else nc - 1 - step
        first = base + chunk * CHUNK
        own = 8 if forward else 0
        buf[own : own + CHUNK, :] = (
            dots(blocks, weight, slice(0, mixing)).astype(BF16).astype(F32)
        )
        z_out[...] = dots(blocks, weight, slice(mixing, mixing + inner)).astype(BF16)

        raw = None
        lo = 0 if forward else 8
        for b in range(mp):
            part = lax.dot_general(
                wdt[lo : lo + 8, b * width : (b + 1) * width],
                blocks[b],
                NT,
                preferred_element_type=F32,
            )
            raw = part if raw is None else raw + part
        raw = raw.astype(BF16).astype(F32)
        raw = jnp.concatenate([raw[:, :SUB], raw[:, SUB:]], axis=0)
        par = head_par[...]
        shifted = raw + par[0:16]
        step_dt = jnp.maximum(shifted, 0.0) + jnp.log1p(jnp.exp(-jnp.abs(shifted)))
        log_decay = step_dt * par[16:32]
        tri = jnp.where(rows <= lanes if forward else rows >= lanes, 1.0, 0.0).astype(F32)
        cum = jnp.dot(
            log_decay, tri, precision=lax.Precision.HIGHEST, preferred_element_type=F32
        )
        total = cum[:, SUB - 1 : SUB] if forward else cum[:, 0:1]
        block_first = first + SUB * (lax.broadcasted_iota(jnp.int32, (16, SUB), 0) // 8)
        position = block_first + lax.broadcasted_iota(jnp.int32, (16, SUB), 1)
        start = piece_start(sm, pieces, position)
        end = piece_end(sm, pieces, position)
        block_last = block_first + SUB - 1
        if forward:
            to_end_ok = end > block_last
            from_start_ok = start < block_first
            whole_ok = piece_start(sm, pieces, block_last) < block_first
        else:
            to_end_ok = start <= block_first
            from_start_ok = end > block_last + 1
            whole_ok = piece_end(sm, pieces, block_first) > block_last + 1
        to_end = jnp.where(to_end_ok, jnp.exp2(total - cum) * step_dt, 0.0)
        from_start = jnp.where(from_start_ok, jnp.exp2(cum), 0.0)
        whole = jnp.where(whole_ok, jnp.exp2(jnp.broadcast_to(total, cum.shape)), 0.0)
        aux_out[0, 0:16, :] = cum
        aux_out[0, 16:32, :] = cum - jnp.log2(step_dt)
        aux_out[0, 32:48, :] = from_start
        aux_out[0, 48:64, :] = whole

        for b in (0, 1) if forward else (1, 0):
            at = first + b * SUB + rows
            if forward:
                room = at - piece_start(sm, pieces, at)
            else:
                room = piece_end(sm, pieces, at) - 1 - at
            same = [None] + [room >= j for j in (1, 2, 3)]
            r0 = own + b * SUB
            out_rows = slice(b * SUB, (b + 1) * SUB)
            for g in range(mixing // 128):
                cols = slice(g * 128, (g + 1) * 128)
                acc = buf[r0 : r0 + SUB, cols] * cw[3:4, cols]
                for j in (1, 2, 3):
                    off = r0 - j if forward else r0 + j
                    tap = buf[off : off + SUB, cols] * cw[3 - j : 4 - j, cols]
                    acc = acc + jnp.where(same[j], tap, 0.0)
                value = silu(acc).astype(BF16)
                if g * 128 < inner:
                    x_out[out_rows, cols] = value
                else:
                    bc_out[out_rows, slice(g * 128 - inner, g * 128 - inner + 128)] = value
            hb = slice(b * 8, b * 8 + 8)
            weights = expand_rows(to_end[hb], e2[...])
            scaled = (x_out[out_rows, :].astype(F32) * weights).astype(BF16)
            added = lax.dot_general(
                bc_out[out_rows, 0:NSTATE], scaled, TN, preferred_element_type=F32
            )
            grow = jnp.sum(whole[hb, 0:1] * e1[...], axis=0, keepdims=True)
            held = state[...]
            before_out[b] = held.astype(BF16)
            state[...] = held * grow + added
            decay[...] = decay[...] * grow

    outs[10][...] = st_f[...]
    outs[11][...] = st_r[...]
    outs[12][...] = dec_f[...]
    outs[13][...] = dec_r[...]


def intra_rows(forward, heads, pieces, sm, x_ref, bc_ref, aux_ref, skip_ref, y_ref, offset, chunk):
    base = sm[pieces] + offset
    rows = lax.broadcasted_iota(jnp.int32, (SUB, SUB), 0)
    lanes = lax.broadcasted_iota(jnp.int32, (SUB, SUB), 1)
    left = lanes < HEAD_DIM
    aux = aux_ref[chunk]
    for b in (0, 1):
        at = pl.ds(pl.multiple_of(chunk * CHUNK + b * SUB, SUB), SUB)
        begin = base + chunk * CHUNK + b * SUB
        if forward:
            mask = (lanes <= rows) & (begin + lanes >= piece_start(sm, pieces, begin + rows))
        else:
            mask = (lanes >= rows) & (begin + lanes < piece_end(sm, pieces, begin + rows))
        scores = lax.dot_general(
            bc_ref[at, NSTATE:], bc_ref[at, 0:NSTATE], NT, preferred_element_type=F32
        )
        cum_t = aux[b * 8 : b * 8 + 8, :].T
        cum_s = aux[16 + b * 8 : 16 + b * 8 + 8, :]
        for pair in range(heads // 2):
            cols = slice(pair * 128, (pair + 1) * 128)
            xf = x_ref[at, cols].astype(F32)
            parts = []
            for h in (2 * pair, 2 * pair + 1):
                gap = jnp.where(mask, cum_t[:, h : h + 1] - cum_s[h : h + 1, :], -1e30)
                parts.append((jnp.exp2(gap) * scores).astype(BF16))
            stacked = jnp.concatenate(
                [
                    jnp.where(left, xf, 0.0).astype(BF16),
                    jnp.where(left, 0.0, xf).astype(BF16),
                ],
                axis=0,
            )
            mixed = jnp.dot(
                jnp.concatenate(parts, axis=1), stacked, preferred_element_type=F32
            )
            y_ref[at, cols] = (mixed + skip_ref[0:1, cols] * xf).astype(BF16)


def rounds_of(count):
    rounds, window = [], 1
    while 4 * window < count - 1:
        rounds.append([window * k for k in (1, 2, 3)])
        window *= 4
    rounds.append([1 + window * k for k in range(-(-(count - 1) // window))])
    return rounds


def exchange_kernel(count, nc, heads, pieces, *refs):
    sm, skip = refs[:2]
    halves = (refs[2:12], refs[12:22])
    mixed = (refs[22:24], refs[24:26])
    into_f, into_r = refs[26:28]
    own, own_fade, held, fade, full = refs[28:33]
    pair_sent, pair_landed, sent, landed, last_sent, last_landed = refs[33:39]
    pair_sems, send_sem, recv_sem, last_sems = refs[39:]
    (st_f0, st_r0, dec_f0, dec_r0), (st_f1, st_r1, dec_f1, dec_r1) = (h[:4] for h in halves)
    index = lax.axis_index("ctx")
    core = lax.rem(index, 2)
    sibling = {"ctx": index + 1 - 2 * core}
    rounds = rounds_of(count // 2)
    signs = (1, -1)
    part = NSTATE // 2
    mine = pl.ds(pl.multiple_of(core * part, part), part)
    theirs = pl.ds(pl.multiple_of((1 - core) * part, part), part)

    def reaches(step):
        return index + step < count if step > 0 else index + step >= 0

    def send(src, dst, send_at, recv_at, target):
        return pltpu.make_async_remote_copy(
            src_ref=src,
            dst_ref=dst,
            send_sem=send_at,
            recv_sem=recv_at,
            device_id=target,
            device_id_type=pl.DeviceIdType.MESH,
        )

    def signal(target):
        pl.semaphore_signal(barrier, inc=1, device_id=target, device_id_type=pl.DeviceIdType.MESH)

    def pack_decay(decay):
        high = decay.astype(BF16)
        return jnp.concatenate([high, (decay - high.astype(F32)).astype(BF16)], axis=0)

    def on_first(shape, yes, no):
        return jnp.where(jnp.full(shape, core, jnp.int32) == 0, yes, no)

    work = [(stream, half) for stream in (0, 1) for half in (0, 1)]

    def compute(pieces_now):
        for stream, half in pieces_now:
            x_ref, bc_ref, aux_ref = halves[half][4 + 3 * stream : 7 + 3 * stream]
            y_ref = mixed[half][stream]

            def body(chunk, carry):
                intra_rows(
                    stream == 0, heads, pieces, sm, x_ref, bc_ref, aux_ref, skip, y_ref,
                    half * nc * CHUNK, chunk,
                )
                return carry

            lax.fori_loop(0, nc, body, 0)

    barrier = pltpu.get_barrier_semaphore()
    steps = sorted({2 * sign * s for r in rounds for s in r for sign in signs})
    signal(sibling)
    for step in steps:

        @pl.when(reaches(step))
        def _(step=step):
            signal({"ctx": index + step})

    peers = 1 + sum(
        1 - lax.div(index + step, count) if step > 0 else lax.div(index + step + count, count)
        for step in steps
    )
    pl.semaphore_wait(barrier, peers)

    own[0] = st_f0[...] * dec_f1[0:1, :] + st_f1[...]
    own[1] = st_r1[...] * dec_r0[0:1, :] + st_r0[...]
    own_fade[0] = dec_f0[...] * dec_f1[...]
    own_fade[1] = dec_r0[...] * dec_r1[...]
    swaps = []
    for stream in (0, 1):
        pair_sent[stream, 0:NSTATE, :] = own[stream].astype(BF16)
        pair_sent[stream, NSTATE : NSTATE + 16, :] = pack_decay(own_fade[stream])
        swap = send(
            pair_sent.at[stream], pair_landed.at[stream],
            pair_sems.at[stream], pair_sems.at[2 + stream], sibling,
        )
        swap.start()
        swaps.append(swap)
    compute(work[0:1])
    for swap in swaps:
        swap.wait()
    shape = held.shape[1:]
    for stream in (0, 1):
        tail = pair_landed[stream, NSTATE : NSTATE + 16, :].astype(F32)
        other_fade = tail[0:8] + tail[8:16]
        other = pair_landed[stream, mine, :].astype(F32)
        here = own[stream, mine, :]
        before = other_fade[0:1] * here + other
        after = own_fade[stream, 0:1, :] * other + here
        held[stream] = on_first(shape, *((before, after) if stream == 0 else (after, before)))
        fade[stream] = own_fade[stream] * other_fade

    slot = 0
    for number, shifts in enumerate(rounds):
        last = number == len(rounds) - 1
        copies = []
        for stream, sign in enumerate(signs):
            at = number * 2 + stream
            sent[at, 0:part, :] = held[stream].astype(BF16)
            sent[at, part : part + 16, :] = pack_decay(fade[stream])
            for s in shifts:
                step = 2 * sign * s
                copy = send(
                    sent.at[at], landed.at[slot],
                    send_sem.at[slot], recv_sem.at[slot], {"ctx": index + step},
                )
                copies.append((stream, step, slot, copy))
                slot += 1

                @pl.when(reaches(step))
                def _(copy=copy):
                    copy.start()

        if len(rounds) == 1:
            compute(work[1:])
        elif number == 0:
            compute(work[1:3])
        elif number == 1:
            compute(work[3:])
        if last:
            held[...] = jnp.zeros_like(held)
            fade[...] = jnp.ones_like(fade)
        for stream, step, at, copy in copies:

            @pl.when(reaches(-step))
            def _(stream=stream, at=at, copy=copy):
                copy.wait_recv()
                more = landed[at, 0:part, :].astype(F32)
                tail = landed[at, part : part + 16, :].astype(F32)
                held[stream] = held[stream] + fade[stream, 0:1, :] * more
                fade[stream] = fade[stream] * (tail[0:8] + tail[8:16])

        for stream, step, at, copy in copies:

            @pl.when(reaches(step))
            def _(copy=copy):
                copy.wait_send()

    swaps = []
    for stream in (0, 1):
        last_sent[stream] = held[stream].astype(BF16)
        swap = send(
            last_sent.at[stream], last_landed.at[stream],
            last_sems.at[stream], last_sems.at[2 + stream], sibling,
        )
        swap.start()
        swaps.append(swap)
    for stream in (0, 1):
        swaps[stream].wait()
        full[stream, mine, :] = held[stream]
        full[stream, theirs, :] = last_landed[stream].astype(F32)
        tail = pair_landed[stream, NSTATE : NSTATE + 16, :].astype(F32)
        outer = full[stream]
        passed = (tail[0:1] + tail[8:9]) * outer + pair_landed[stream, 0:NSTATE, :].astype(F32)
        into = on_first(
            outer.shape, *((outer, passed) if stream == 0 else (passed, outer))
        )
        if stream == 0:
            into_f[0] = into
            into_f[1] = st_f0[...] + dec_f0[0:1, :] * into
        else:
            into_r[0] = st_r1[...] + dec_r1[0:1, :] * into
            into_r[1] = into


def finish_kernel(nc, inner, *refs):
    ins, par = refs[0:12], refs[12:15]
    outs = refs[15:19]
    grown = refs[19:21]
    gain_ref, e1, e2 = par
    step = pl.program_id(0)

    @pl.when(step == 0)
    def _():
        grown[0][...] = jnp.ones_like(grown[0])
        grown[1][...] = jnp.ones_like(grown[1])

    ones = jnp.ones((8, inner), BF16)
    for stream in (0, 1):
        y_ref, z_ref, bc_ref, aux_ref, before_ref, into_ref = ins[stream * 6 : stream * 6 + 6]
        g_out, ss_out = outs[stream * 2 : stream * 2 + 2]
        into = into_ref[...]
        for b in (0, 1) if stream == 0 else (1, 0):
            at = slice(b * SUB, (b + 1) * SUB)
            grow = grown[stream][...]
            state = (before_ref[b].astype(F32) + grow * into).astype(BF16)
            factor = expand_rows(aux_ref[0, 32 + b * 8 : 40 + b * 8, :], e2[...])
            inter = jnp.dot(bc_ref[at, NSTATE:], state, preferred_element_type=F32)
            mixed = y_ref[at, :].astype(F32) + inter * factor
            gated = mixed * silu(z_ref[at, :].astype(F32))
            ss_out[:, at] = lax.dot_general(
                ones, (gated * gated).astype(BF16), NT, preferred_element_type=F32
            )
            g_out[at, :] = (gated * gain_ref[0:1, :]).astype(BF16)
            whole = aux_ref[0, 48 + b * 8 : 56 + b * 8, 0:1]
            grown[stream][...] = grow * jnp.sum(whole * e1[...], axis=0, keepdims=True)


def output_kernel(mp, total_width, ss_ref, gf_ref, gr_ref, wf_ref, wr_ref, *outs):
    factor = lax.rsqrt(ss_ref[...] * (1.0 / total_width) + EPSILON).T
    width = wf_ref.shape[1] // mp
    for k in range(mp):
        cols = slice(k * width, (k + 1) * width)
        part = factor[:, 0:1] * jnp.dot(gf_ref[...], wf_ref[:, cols], preferred_element_type=F32)
        part = part + factor[:, 4:5] * jnp.dot(
            gr_ref[...], wr_ref[:, cols], preferred_element_type=F32
        )
        outs[k][...] = part.astype(outs[k].dtype)


def shift(value, axis, by, wrap):
    count = lax.axis_size(axis)
    if wrap:
        pairs = [(i, (i + by) % count) for i in range(count)]
    else:
        pairs = [(i, i + by) for i in range(count) if 0 <= i + by < count]
    return lax.ppermute(value, axis, pairs)


def cost(flops, size, trans=0):
    return pl.CostEstimate(flops=flops, bytes_accessed=size, transcendentals=trans)


def shards(
    hidden, w_x, w_z, w_bc, w_dt, conv_x, conv_bc, dt_bias, decay_rate, skip_gain, norm_gain,
    w_out, piece_lengths,
):
    mp = lax.axis_size("mp")
    me = lax.axis_index("mp")
    rows, width = hidden.shape
    model = width * mp
    heads = dt_bias.shape[0]
    inner = heads * HEAD_DIM
    mixing = inner + 2 * NSTATE
    pieces = piece_lengths.shape[0]
    part_rows = rows // 2
    nc = part_rows // CHUNK
    params = pltpu.CompilerParams(vmem_limit_bytes=VMEM_LIMIT)

    from_below = shift(hidden[rows - 16 :], "ctx", 1, False)
    from_above = shift(hidden[:16], "ctx", -1, False)
    halo_own = jnp.concatenate(
        [
            from_below,
            hidden[part_rows : part_rows + 16],
            hidden[part_rows - 16 : part_rows],
            from_above,
        ],
        axis=0,
    )
    halos = [halo_own] + [shift(halo_own, "mp", k, True) for k in range(1, mp)]
    lower, upper = hidden[:part_rows], hidden[part_rows:]
    low_blocks = [shift(lower, "mp", k, True) for k in range(1, mp)]
    upper, *low_blocks = lax.optimization_barrier((upper, *low_blocks))
    high_blocks = [shift(upper, "mp", k, True) for k in range(1, mp)]
    blocks = ([lower] + low_blocks, [upper] + high_blocks)

    place = jnp.arange(model, dtype=jnp.int32)
    came = lax.rem(me - place // width + mp, mp) * width + lax.rem(place, width)
    columns = jnp.arange(model, dtype=jnp.int32)[None, :]
    pick_f = (came[:, None] == columns).astype(BF16)
    pick_r = (model - 1 - came[:, None] == columns).astype(BF16)
    w_in = jnp.concatenate([w_x, w_bc, w_z], axis=1)
    w_f = jnp.dot(pick_f, w_in, preferred_element_type=F32).astype(BF16)
    w_r = jnp.dot(pick_r, w_in, preferred_element_type=F32).astype(BF16)
    pad = 8 - heads
    dt_pad = jnp.pad(w_dt, ((0, 0), (0, pad)))
    dt_t = lax.dot_general(
        dt_pad,
        jnp.concatenate([pick_f, pick_r], axis=0),
        (((0,), (1,)), ((), ())),
        preferred_element_type=F32,
    ).astype(BF16)
    w_dt2 = jnp.concatenate([dt_t[:, :model], dt_t[:, model:]], axis=0)
    goes = lax.rem(me + place // width, mp) * width + lax.rem(place, width)
    out_f = jnp.dot(
        w_out, (columns.T == goes[None, :]).astype(BF16), preferred_element_type=F32
    ).astype(BF16)
    out_r = jnp.dot(
        w_out, (columns.T == model - 1 - goes[None, :]).astype(BF16), preferred_element_type=F32
    ).astype(BF16)

    bounds = jnp.cumsum(piece_lengths).astype(jnp.int32)
    first_row = (lax.axis_index("ctx") * rows).astype(jnp.int32)[None]
    sms = [jnp.concatenate([bounds, first_row + half * part_rows]) for half in (0, 1)]
    conv_w = jnp.pad(jnp.concatenate([conv_x, conv_bc], axis=1), ((0, 4), (0, 0)))
    bias = jnp.pad(dt_bias, (0, pad))
    rate = jnp.pad(-LOG2E * decay_rate, (0, pad))
    head_par = jnp.broadcast_to(
        jnp.concatenate([bias, bias, rate, rate])[:, None], (32, SUB)
    ).astype(F32)
    owner = jnp.arange(inner, dtype=jnp.int32)[None, :] // HEAD_DIM
    e1 = (jnp.arange(8, dtype=jnp.int32)[:, None] == owner).astype(F32)
    e2 = jnp.concatenate([e1, e1], axis=0).astype(BF16)
    skip8 = jnp.broadcast_to(jnp.repeat(skip_gain, HEAD_DIM)[None, :], (8, inner))
    gain8 = jnp.broadcast_to(norm_gain[None, :], (8, inner))

    smem = pl.BlockSpec(memory_space=pltpu.SMEM)

    def whole(shape):
        return pl.BlockSpec(shape, lambda i: (0,) * len(shape))

    def up(cols):
        return pl.BlockSpec((CHUNK, cols), lambda i: (i, 0))

    def down(cols):
        return pl.BlockSpec((CHUNK, cols), lambda i: (nc - 1 - i, 0))

    aux_up = pl.BlockSpec((1, 64, SUB), lambda i: (i, 0, 0))
    aux_down = pl.BlockSpec((1, 64, SUB), lambda i: (nc - 1 - i, 0, 0))
    st_up = pl.BlockSpec((2, NSTATE, inner), lambda i: (i, 0, 0))
    st_down = pl.BlockSpec((2, NSTATE, inner), lambda i: (nc - 1 - i, 0, 0))

    def sds(shape, dtype):
        return jax.ShapeDtypeStruct(shape, dtype)

    stream_shapes = [
        sds((part_rows, inner), BF16),
        sds((part_rows, 2 * NSTATE), BF16),
        sds((part_rows, inner), BF16),
        sds((nc, 64, SUB), F32),
        sds((2 * nc, NSTATE, inner), BF16),
    ]
    project = pl.pallas_call(
        functools.partial(project_kernel, nc, mp, inner, pieces),
        grid=(nc,),
        in_specs=[smem]
        + [up(width)] * mp
        + [down(width)] * mp
        + [whole((32, width))] * mp
        + [
            whole((model, mixing + inner)),
            whole((model, mixing + inner)),
            whole((16, model)),
            whole((8, mixing)),
            whole((32, SUB)),
            whole((8, inner)),
            whole((16, inner)),
        ],
        out_specs=[up(inner), up(2 * NSTATE), up(inner), aux_up, st_up]
        + [down(inner), down(2 * NSTATE), down(inner), aux_down, st_down]
        + [whole((NSTATE, inner))] * 2
        + [whole((8, inner))] * 2,
        out_shape=stream_shapes
        + stream_shapes
        + [sds((NSTATE, inner), F32)] * 2
        + [sds((8, inner), F32)] * 2,
        scratch_shapes=[
            pltpu.VMEM((CHUNK + 8, mixing), F32),
            pltpu.VMEM((CHUNK + 8, mixing), F32),
            pltpu.VMEM((NSTATE, inner), F32),
            pltpu.VMEM((NSTATE, inner), F32),
            pltpu.VMEM((8, inner), F32),
            pltpu.VMEM((8, inner), F32),
        ],
        compiler_params=params,
        cost_estimate=cost(4 * part_rows * model * (mixing + inner), 10 << 20),
        name="project",
    )
    made = [
        project(
            sms[half], *blocks[half], *blocks[half],
            *[h[half * 32 : half * 32 + 32] for h in halos],
            w_f, w_r, w_dt2, conv_w, head_par, e1, e2,
        )
        for half in (0, 1)
    ]

    count = lax.axis_size("ctx")
    rounds = rounds_of(count // 2)
    slots = 2 * sum(len(r) for r in rounds)
    packed = NSTATE // 2 + 16
    vmem = pl.BlockSpec(memory_space=pltpu.VMEM)
    *mixed, into_f, into_r = pl.pallas_call(
        functools.partial(exchange_kernel, count, nc, heads, pieces),
        in_specs=[smem] + [vmem] * 21,
        out_specs=[vmem] * 6,
        out_shape=[sds((part_rows, inner), BF16)] * 4 + [sds((2, NSTATE, inner), F32)] * 2,
        scratch_shapes=[
            pltpu.VMEM((2, NSTATE, inner), F32),
            pltpu.VMEM((2, 8, inner), F32),
            pltpu.VMEM((2, NSTATE // 2, inner), F32),
            pltpu.VMEM((2, 8, inner), F32),
            pltpu.VMEM((2, NSTATE, inner), F32),
            pltpu.VMEM((2, NSTATE + 16, inner), BF16),
            pltpu.VMEM((2, NSTATE + 16, inner), BF16),
            pltpu.VMEM((2 * len(rounds), packed, inner), BF16),
            pltpu.VMEM((slots, packed, inner), BF16),
            pltpu.VMEM((2, NSTATE // 2, inner), BF16),
            pltpu.VMEM((2, NSTATE // 2, inner), BF16),
            pltpu.SemaphoreType.DMA((4,)),
            pltpu.SemaphoreType.DMA((slots,)),
            pltpu.SemaphoreType.DMA((slots,)),
            pltpu.SemaphoreType.DMA((4,)),
        ],
        compiler_params=pltpu.CompilerParams(
            vmem_limit_bytes=VMEM_LIMIT, collective_id=0, has_side_effects=True
        ),
        cost_estimate=cost(40 * rows * SUB * inner, 16 << 20, 2 * rows * SUB * heads),
        name="exchange",
    )(
        sms[0],
        skip8,
        *[
            value
            for m in made
            for value in (*m[10:14], m[0], m[1], m[3], m[5], m[6], m[8])
        ],
    )

    finish = pl.pallas_call(
        functools.partial(finish_kernel, nc, inner),
        grid=(nc,),
        in_specs=[up(inner), up(inner), up(2 * NSTATE), aux_up, st_up, whole((NSTATE, inner))]
        + [down(inner), down(inner), down(2 * NSTATE), aux_down, st_down, whole((NSTATE, inner))]
        + [whole((8, inner)), whole((8, inner)), whole((16, inner))],
        out_specs=[
            up(inner),
            pl.BlockSpec((8, CHUNK), lambda i: (0, i)),
            down(inner),
            pl.BlockSpec((8, CHUNK), lambda i: (0, nc - 1 - i)),
        ],
        out_shape=[sds((part_rows, inner), BF16), sds((8, part_rows), F32)] * 2,
        scratch_shapes=[pltpu.VMEM((1, inner), F32)] * 2,
        compiler_params=params,
        cost_estimate=cost(4 * part_rows * NSTATE * inner, 12 << 20),
        name="finish",
    )
    output = pl.pallas_call(
        functools.partial(output_kernel, mp, inner * mp),
        grid=(nc,),
        in_specs=[
            pl.BlockSpec((8, CHUNK), lambda i: (0, i)),
            up(inner),
            up(inner),
            whole((inner, model)),
            whole((inner, model)),
        ],
        out_specs=[up(width)] * mp,
        out_shape=[sds((part_rows, width), F32)] + [sds((part_rows, width), BF16)] * (mp - 1),
        compiler_params=params,
        cost_estimate=cost(4 * part_rows * inner * model, 4 << 20),
        name="output",
    )
    forward_rows = jnp.arange(8, dtype=jnp.int32)[:, None] < 4
    gated, squares = [], []
    mixed_now = mixed[0:2]
    for half, m in enumerate(made):
        gated_f, square_f, gated_r, square_r = finish(
            mixed_now[0], m[2], m[1], m[3], m[4], into_f[half],
            mixed_now[1], m[7], m[6], m[8], m[9], into_r[half],
            gain8, e1, e2,
        )
        gated.append((gated_f, gated_r))
        square = jnp.where(forward_rows, square_f, square_r)
        if half == 0:
            square, mixed_now = lax.optimization_barrier((square, mixed[2:4]))
        squares.append(square)
    other = [[shift(sq, "mp", k, True) for k in range(1, mp)] for sq in squares]
    totals = [sum(got, sq) for got, sq in zip(other, squares)]
    first = output(totals[0], *gated[0], out_f, out_r)
    first, totals[1] = lax.optimization_barrier((first, totals[1]))
    results = []
    for parts in (first, output(totals[1], *gated[1], out_f, out_r)):
        result = parts[0]
        for k in range(1, mp):
            result = result + shift(parts[k], "mp", k, True).astype(F32)
        results.append(result.astype(BF16))
    return jnp.concatenate(results, axis=0)


def solution(mesh):
    return jax.shard_map(
        shards,
        mesh=mesh,
        in_specs=(
            P("ctx", "mp"), P(None, "mp"), P(None, "mp"), P(), P(None, "mp"), P(None, "mp"), P(),
            P("mp"), P("mp"), P("mp"), P("mp"), P("mp", None), P(),
        ),
        out_specs=P("ctx", "mp"),
        check_vma=False,
    )
```
